512 devices in a mesh: tile: 32 (over y, z_lo, core), trc: 16 (over x, z_hi).
Axes of the slice: x: 4, y: 8, z: 8 (z_hi: 4, z_lo: 2; z = z_hi * 2 + z_lo), core: 2. Of those that a mesh axis runs over, the one named last changes fastest.
Arguments:
- tracers: float32 [512, 128, 2, 128], P('trc', 'tile'), may hold values from 0.05 to 2
- courant: float32 [3, 128, 2, 128], P(None, 'tile', None, 'trc'), may hold values from -6 to 6
- shear: float32 [3, 128, 2, 128], P(None, 'tile', None, 'trc'), may hold values from -8 to 8
- offsets: int32 [3, 128, 2, 128], P(None, 'tile'), may hold values from -1 to 0
- seam_flips: int32 [32], replicated, may hold values from 0 to 1
- kernel: float32 [32, 32], replicated, may hold values from 0.0005 to 0.004
- coag_target: int32 [32, 32], replicated, may hold values from 0 to 31, as said below
Outputs:
- updated: float32 [512, 128, 2, 128], P('trc', 'tile')
The draws below stay inside these ranges and needn't reach their ends.
Inputs may be any that keep to these rules, and one draw needn't show every extreme that they name: coag_target[i, j] lies between max(i, j) and 31.
All inputs are finite; a program needn't handle non-finite values.
Results may differ from the reference program's by a relative error of at most 0.00014.
Values sent between devices are 32-bit elements; how exact they have to be, the bound alone decides.
A program may use at most 64 MiB of HBM per device.

```python
import math
import jax
import jax.numpy as jnp
from jax import lax

BINS = 32
COMPS = 16
ITER = 3
XW = 4
LEV = 2
YW = 128
TRACERS = 512
NX = 128
N_TILE = 32


def draw_coag_target(key, part):
    bin_index = jnp.arange(BINS, dtype=jnp.int32)
    floor_bin = jnp.maximum(bin_index[:, None], bin_index[None, :])
    return floor_bin + jax.random.randint(key, (BINS, BINS), 0, BINS - floor_bin)


def set_ends(drawn, rng, smallest, largest):
    longest = drawn.shape.index(max(drawn.shape))
    spots = []
    for shift in (0, 1):
        where = [jax.random.randint(jax.random.fold_in(rng, axis), (), 0, length) for axis, length in enumerate(drawn.shape)]
        where[longest] = (where[longest] + shift) % drawn.shape[longest]
        spots.append(tuple(where))
    return drawn.at[spots[0]].set(smallest).at[spots[1]].set(largest)


def level_of(own_key, dims, shards, low, largest):
    factor_of = 1.0
    for axis_at, shards_of in shards:
        heights = jax.random.uniform(jax.random.fold_in(jax.random.fold_in(own_key, 6), axis_at), (shards_of,), jnp.float32, low / len(shards), largest / len(shards))
        factor_of = factor_of * jnp.repeat(jnp.exp(heights), dims[axis_at] // shards_of).reshape((-1,) + (1,) * (len(dims) - 1 - axis_at))
    return factor_of


def gaussian(stream_key, extent, spread, reach, pieces=(), kind=jnp.bfloat16):
    drawn = spread * jax.random.normal(stream_key, extent, jnp.float32)
    if pieces:
        drawn = drawn * level_of(stream_key, extent, pieces, -0.22, 0.18)
    return jnp.clip(drawn, -reach, reach).astype(kind)


def setup_inputs(seed: int = 0) -> dict:
    keys = jax.random.split(jax.random.key(seed), 8)
    return {
        "tracers": jnp.clip(jnp.exp(math.log(2.0) - 3.6888794 * jax.random.uniform(keys[0], (TRACERS, NX, LEV, YW), jnp.float32) ** level_of(keys[0], (TRACERS, NX, LEV, YW), ((0, 16), (1, 32)), -0.2, 0.2)), 0.05, 2.0),
        "courant": gaussian(keys[1], (3, NX, LEV, YW), 1.5, 6.0, ((1, 32), (3, 16)), jnp.float32),
        "shear": gaussian(keys[2], (3, NX, LEV, YW), 2.0, 8.0, ((1, 32), (3, 16)), jnp.float32),
        "offsets": set_ends(jax.random.randint(keys[3], (3, NX, LEV, YW), -1, 1), jax.random.fold_in(keys[3], 1), -1, 0).astype(jnp.int32),
        "seam_flips": set_ends(jax.random.randint(keys[4], (N_TILE,), 0, 2), jax.random.fold_in(keys[4], 1), 0, 1).astype(jnp.int32),
        "kernel": jnp.clip(jnp.exp(jax.random.uniform(keys[5], (BINS, BINS), jnp.float32, math.log(0.0005), math.log(0.004))), 0.0005, 0.004),
        "coag_target": draw_coag_target(jax.random.fold_in(keys[7], 71), 0),
    }


precise = lax.Precision.HIGHEST


def fractions(courant, shear):
    fraction = jnp.full(courant.shape, 0.5, jnp.float32)
    for repeat in range(ITER):
        fraction = jax.nn.sigmoid(courant + shear * (fraction - 0.5))
    return fraction


def cubic_taps(fraction, offsets):
    first_node = -fraction * (fraction - 1.0) * (fraction - 2.0) / 6.0
    second_node = (fraction + 1.0) * (fraction - 1.0) * (fraction - 2.0) / 2.0
    third_node = -(fraction + 1.0) * fraction * (fraction - 2.0) / 2.0
    fourth_node = (fraction + 1.0) * fraction * (fraction - 1.0) / 6.0
    zeros = jnp.zeros_like(fraction)
    lower = offsets == -1
    weights = [jnp.where(lower, first_node, zeros), jnp.where(lower, second_node, first_node),
               jnp.where(lower, third_node, second_node), jnp.where(lower, fourth_node, third_node),
               jnp.where(lower, zeros, fourth_node)]
    return jnp.stack(weights, axis=1)


def interpolate(padded, stencil):
    cross, levels, along = stencil.shape[2], stencil.shape[3], stencil.shape[4]
    summed = jnp.zeros((padded.shape[0], cross, levels, along), jnp.float32)
    for x_step in range(5):
        for l_step in range(5):
            partial_sum = jnp.zeros((padded.shape[0], cross, levels, along), jnp.float32)
            for y_step in range(5):
                partial_sum = partial_sum + stencil[2, y_step] * padded[:, x_step:x_step + cross, l_step:l_step + levels, y_step:y_step + along]
            summed = summed + (stencil[0, x_step] * stencil[1, l_step]) * partial_sum
    return summed


def seam_pad(stacked, seam_flips):
    left_rim = jnp.roll(stacked, 1, axis=0)[:, :, -2:]
    right_rim = jnp.roll(stacked, -1, axis=0)[:, :, :2]
    left_flag = (seam_flips == 1)[:, None, None, None, None]
    right_flag = (jnp.roll(seam_flips, -1) == 1)[:, None, None, None, None]
    left_rim = jnp.where(left_flag, left_rim[..., ::-1], left_rim)
    right_rim = jnp.where(right_flag, right_rim[..., ::-1], right_rim)
    widened = jnp.concatenate([left_rim, stacked, right_rim], axis=2)
    widened = jnp.pad(widened, ((0, 0), (0, 0), (0, 0), (2, 2), (0, 0)), mode="edge")
    return jnp.pad(widened, ((0, 0), (0, 0), (0, 0), (0, 0), (2, 2)), mode="wrap")


def coagulate(masses, kernel, coag_target):
    number = jnp.sum(jnp.abs(masses), axis=1)
    losses = jnp.dot(kernel, number, precision=precise, preferred_element_type=jnp.float32)
    bin_index = jnp.arange(BINS, dtype=jnp.int32)
    matches = (coag_target[None, :, :] == bin_index[:, None, None]).astype(jnp.float32)
    redistribute = (matches * kernel[None, :, :]).reshape(BINS * BINS, BINS)
    transfer_rate = jnp.dot(redistribute, number, precision=precise, preferred_element_type=jnp.float32)
    transfer_rate = transfer_rate.reshape(BINS, BINS, number.shape[1])
    gained = jnp.einsum("bic,ikc->bkc", transfer_rate, masses, precision=precise)
    return (masses + gained) / (1.0 + losses[:, None, :])


def reference(tracers, courant, shear, offsets, seam_flips, kernel, coag_target):
    stencil = cubic_taps(fractions(courant, shear), offsets)
    stencil = stencil.reshape(3, 5, N_TILE, XW, LEV, YW).transpose(2, 0, 1, 3, 4, 5)
    stacked = tracers.reshape(TRACERS, N_TILE, XW, LEV, YW).transpose(1, 0, 2, 3, 4)

    def one_tile(operands):
        return interpolate(operands[0], operands[1])

    for repeat in range(2):
        padded = seam_pad(stacked, seam_flips)
        stacked = lax.map(one_tile, (padded, stencil))
    masses = stacked.reshape(N_TILE, BINS, COMPS, XW * LEV * YW)

    def one_block(block):
        return coagulate(block, kernel, coag_target)

    masses = lax.map(one_block, masses)
    masses = masses.reshape(N_TILE, TRACERS, XW, LEV, YW).transpose(1, 0, 2, 3, 4)
    return masses.reshape(TRACERS, NX, LEV, YW)
```

```python
import functools

import jax
import jax.numpy as jnp
from jax import lax
from jax.experimental import pallas as pl
from jax.experimental.pallas import tpu as pltpu
from jax.sharding import PartitionSpec as P

BINS = 32
COMPS = 16
ITER = 3
TRC = 16
SIDE = 4
MESH = pl.DeviceIdType.MESH
EXACT = lax.Precision.HIGHEST


def taps(f, lower):
    p0 = -f * (f - 1.0) * (f - 2.0) / 6.0
    p1 = (f + 1.0) * (f - 1.0) * (f - 2.0) / 2.0
    p2 = -(f + 1.0) * f * (f - 2.0) / 2.0
    p3 = (f + 1.0) * f * (f - 1.0) / 6.0
    zero = jnp.zeros_like(f)
    return [
        jnp.where(lower, p0, zero),
        jnp.where(lower, p1, p0),
        jnp.where(lower, p2, p1),
        jnp.where(lower, p3, p2),
        jnp.where(lower, zero, p3),
    ]


def transport(src, wbuf, x):
    out = None
    for b in range(5):
        acc = [[None] * 4, [None] * 4]
        for a in range(5):
            for level in range(2):
                q = [src[2 * x + 2 * a + level, pl.ds(8 * g, 8), :] for g in range(4)]
                for l in range(2):
                    w = wbuf[(b * 5 + a) * 2 + level, pl.ds(2 * x + l, 1), :]
                    w = jnp.broadcast_to(w, (8, 128))
                    for g in range(4):
                        term = w * q[g]
                        acc[l][g] = term if acc[l][g] is None else acc[l][g] + term
        if b != 2:
            acc = [[pltpu.roll(v, (2 - b) % 128, 1) for v in row] for row in acc]
        out = acc if out is None else [[o + v for o, v in zip(r, s)] for r, s in zip(out, acc)]
    return out


def body(
    n_tile, tr, co, sh, of, fl, ke, ct, out,
    tin, cin, sin, oin, kin, ctin, fpad, fsend, frecv, wbuf, src1, src2,
    send2, recv2, abuf, nbuf, tbuf, rbuf, send3, recv3,
    in_sem, hs_sem, hr_sem, fs_sem, fr_sem, s2_sem, r2_sem, s3_sem, r3_sem,
):
    tile, me = lax.axis_index("tile"), lax.axis_index("trc")
    x_me, z_me = me // SIDE, lax.rem(me, SIDE)
    prev = lax.rem(tile + n_tile - 1, n_tile)
    after = lax.rem(tile + 1, n_tile)

    loads = [
        pltpu.make_async_copy(s, d, in_sem.at[i])
        for i, (s, d) in enumerate(
            ((co, cin), (sh, sin), (tr, tin), (of, oin), (ke, kin), (ct, ctin))
        )
    ]
    for load in loads:
        load.start()

    barrier = pltpu.get_barrier_semaphore()
    for k in range(1, TRC):
        pl.semaphore_signal(barrier, inc=1, device_id=(tile, lax.rem(me + k, TRC)), device_id_type=MESH)
    for t in (prev, after):
        pl.semaphore_signal(barrier, inc=1, device_id=(t, me), device_id_type=MESH)

    lane = lax.broadcasted_iota(jnp.int32, (8, 128), 1)
    sub = lax.broadcasted_iota(jnp.int32, (8, 128), 0)
    low = lane < 64

    fpad[...] = jnp.zeros_like(fpad)
    loads[0].wait()
    loads[1].wait()
    c, s = cin[...], sin[...]
    f = jnp.full(c.shape, 0.5, jnp.float32)
    for _ in range(ITER):
        f = jax.nn.sigmoid(c + s * (f - 0.5))
    fpad[:, 0:8] = f
    zero = jnp.zeros((8, 128), jnp.float32)
    rows = []
    for packed in (fpad[0:8] + pltpu.roll(fpad[8:16], 8, 1), fpad[16:24]):
        for bit in (1, 2, 4):
            packed = jnp.where(lax.rem(sub // bit, 2) == 1, pltpu.roll(packed, 128 - 16 * bit, 1), packed)
        packed = pltpu.roll(packed, me * 8, 1)
        rows.append(jnp.sum(packed, axis=0, keepdims=True))
    top, bottom = rows
    fsend[0:1, :] = top
    fsend[1:2, :] = bottom
    frecv[me, 0:1, :] = top
    frecv[me, 1:2, :] = bottom

    loads[2].wait()
    for r in range(8):
        for g in range(4):
            src1[4 + r, pl.ds(8 * g, 8), :] = tin[pl.ds(64 * g + r, 8, stride=8), :]

    pl.semaphore_wait(barrier, TRC + 1)

    def halo(buf, phase, side):
        return pltpu.make_async_remote_copy(
            src_ref=buf.at[pl.ds(4 + 4 * side, 4)],
            dst_ref=buf.at[pl.ds(12 - 12 * side, 4)],
            send_sem=hs_sem.at[phase, side],
            recv_sem=hr_sem.at[phase, side],
            device_id=((prev, after)[side], me),
            device_id_type=MESH,
        )

    def share(dest):
        return pltpu.make_async_remote_copy(
            src_ref=fsend, dst_ref=frecv.at[me], send_sem=fs_sem.at[dest], recv_sem=fr_sem.at[me],
            device_id=(tile, dest), device_id_type=MESH,
        )

    def spread(src, dst, s_sem, r_sem, dest):
        return pltpu.make_async_remote_copy(
            src_ref=src.at[dest], dst_ref=dst.at[me], send_sem=s_sem.at[dest], recv_sem=r_sem.at[me],
            device_id=(tile, dest), device_id_type=MESH,
        )

    def arrived(dst, r_sem, s_sem, source):
        return pltpu.make_async_remote_copy(
            src_ref=dst.at[source], dst_ref=dst.at[source], send_sem=s_sem.at[source],
            recv_sem=r_sem.at[source], device_id=(tile, source), device_id_type=MESH,
        )

    others = [lax.rem(me + k, TRC) for k in range(1, TRC)]
    for dest in others:
        share(dest).start()
    halo(src1, 0, 0).start()
    halo(src1, 0, 1).start()

    loads[4].wait()
    loads[5].wait()
    spot = lax.broadcasted_iota(jnp.int32, (32, 256), 1)
    j = lax.broadcasted_iota(jnp.int32, (32, 256), 0)
    at = lax.rem(j, 2) * 16 + j // 2
    rate = jnp.zeros((16, 256), jnp.float32)
    target = jnp.zeros((16, 256), jnp.float32)
    for p in range(2):
        place = (lax.rem(spot, 64) == at + 32 * p).astype(jnp.float32)
        rate += jnp.dot(kin[pl.ds(p, 16, stride=2), :], place, precision=EXACT, preferred_element_type=jnp.float32)
        target += jnp.dot(
            ctin[pl.ds(p, 16, stride=2), :].astype(jnp.float32), place, precision=EXACT,
            preferred_element_type=jnp.float32,
        )
    coarse = rate.astype(jnp.bfloat16).astype(jnp.float32)
    rate = jnp.where(lax.broadcasted_iota(jnp.int32, (16, 256), 1) < 128, coarse, rate - coarse)

    def fill(b, carry):
        hit = jnp.abs(target - b.astype(jnp.float32)) < 0.5
        abuf[b] = jnp.where(hit, rate, 0.0).astype(jnp.bfloat16)
        return carry

    lax.fori_loop(0, BINS, fill, 0)
    abuf[BINS] = rate.astype(jnp.bfloat16)

    loads[3].wait()
    for source in others:
        arrived(frecv, fr_sem, fs_sem, source).wait_recv()
    place = lax.rem(lane // 8 + 2 * sub, 16)
    spots = [place, lax.rem(place + 15, 16), place]
    frac = [zero, zero, zero]
    for source in range(TRC):
        rows = [jnp.broadcast_to(frecv[source, i : i + 1, :], (8, 128)) for i in (0, 0, 1)]
        frac = [jnp.where(spots[d] == source, rows[d], frac[d]) for d in range(3)]
    frac[1] = pltpu.roll(frac[1], 120, 1)
    weights = []
    for d in range(3):
        fd = pltpu.roll(frac[d], 0, 1, stride=16, stride_axis=0)
        weights.append(taps(fd, oin[8 * d : 8 * d + 8, :] == -1))
    cross, levels, along = weights
    upper = lax.rem(sub, 2) == 1
    level0 = levels[0] + levels[1] + jnp.where(upper, zero, levels[2])
    level1 = levels[3] + levels[4] + jnp.where(upper, levels[2], zero)
    for a in range(5):
        for level, lw in enumerate((level0, level1)):
            pair = cross[a] * lw
            for b in range(5):
                w = pair * along[b]
                if b != 2:
                    w = pltpu.roll(w, (b - 2) % 128, 1)
                wbuf[(b * 5 + a) * 2 + level] = w

    flags = (fl[tile], fl[after])
    mirror = 127 - lane

    def turn(buf, side):
        turned = jnp.full((8, 128), flags[side], jnp.int32) == 1

        def one(i, carry):
            for g in range(4):
                at = (12 * side + i, pl.ds(8 * g, 8), slice(None))
                v = buf[at]
                buf[at] = jnp.where(turned, jnp.take_along_axis(v, mirror, axis=1), v)
            return carry

        lax.fori_loop(0, 4, one, 0)

    def rims(buf, phase):
        for side in (1, 0):
            halo(buf, phase, side).wait_recv()
            turn(buf, 1 - side)

    rims(src1, 0)

    def first(x, carry):
        moved = transport(src1, wbuf, x)
        for l in range(2):
            for g in range(4):
                src2[4 + 2 * x + l, pl.ds(8 * g, 8), :] = moved[l][g]
        return carry

    lax.fori_loop(0, 2, first, 0)
    halo(src2, 1, 0).start()
    lax.fori_loop(2, 4, first, 0)
    halo(src2, 1, 1).start()
    rims(src2, 1)

    def second(k, carry):
        x = lax.rem(x_me + 1 + k, SIDE)
        moved = transport(src2, wbuf, x)
        for l in range(2):
            for g in range(2):
                even, odd = moved[l][g], moved[l][2 + g]
                at = pl.ds(8 * g, 8)
                send2[4 * x + 2 * l, at, :] = jnp.where(low, even, pltpu.roll(odd, 64, 1))
                send2[4 * x + 2 * l + 1, at, :] = jnp.where(low, pltpu.roll(even, 64, 1), odd)
        for i in range(1, SIDE):
            spread(send2, recv2, s2_sem, r2_sem, 4 * x + lax.rem(z_me + i, SIDE)).start()

        @pl.when(k < SIDE - 1)
        def _():
            spread(send2, recv2, s2_sem, r2_sem, 4 * x + z_me).start()

        return carry

    lax.fori_loop(0, SIDE, second, 0)
    recv2[me] = send2[me]
    for source in others:
        arrived(recv2, r2_sem, s2_sem, source).wait_recv()

    number = jnp.sum(jnp.abs(recv2[...]), axis=1)
    low16 = lax.broadcasted_iota(jnp.int32, (16, 128), 1) < 64
    other = pltpu.roll(number, 64, 1)
    none = jnp.zeros_like(number)
    nums = jnp.concatenate(
        [
            jnp.where(low16, number, none),
            jnp.where(low16, other, none),
            jnp.where(low16, none, other),
            jnp.where(low16, none, number),
        ],
        axis=0,
    )
    coarse = nums.astype(jnp.bfloat16)
    fine = (nums - coarse.astype(jnp.float32)).astype(jnp.bfloat16)
    nums = jnp.concatenate([coarse, fine, coarse, fine], axis=0)
    rates = jnp.dot(
        abuf[...].reshape((BINS + 1) * 16, 256), nums, preferred_element_type=jnp.float32
    )
    tbuf[...] = rates.reshape(BINS + 1, 16, 128)
    rbuf[...] = 1.0 / (1.0 + tbuf[BINS])

    def gain(k, carry):
        step = lax.rem(k + 1, TRC)
        g = lax.rem(x_me + step // SIDE, SIDE) * SIDE + lax.rem(z_me + step, SIDE)
        acc = [[None, None], [None, None]]
        for i in range(TRC):
            m = [recv2[i, 0:8, :], recv2[i, 8:16, :]]
            for p in range(2):
                t = jnp.broadcast_to(tbuf[2 * g + p, i : i + 1, :], (8, 128))
                for h in range(2):
                    term = t * m[h]
                    acc[p][h] = term if acc[p][h] is None else acc[p][h] + term
        rec = jnp.broadcast_to(rbuf[pl.ds(g, 1), :], (8, 128))
        for h in range(2):
            gained = jnp.where(low, acc[0][h], acc[1][h]) + pltpu.roll(jnp.where(low, acc[1][h], acc[0][h]), 64, 1)
            send3[g, 8 * h : 8 * h + 8, :] = (recv2[g, 8 * h : 8 * h + 8, :] + gained) * rec

        @pl.when(k < TRC - 1)
        def _():
            spread(send3, recv3, s3_sem, r3_sem, g).start()

        return carry

    lax.fori_loop(0, TRC, gain, 0)
    recv3[me] = send3[me]
    for source in others:
        arrived(recv3, r3_sem, s3_sem, source).wait_recv()
    for r in range(8):
        for h in range(2):
            c0, c1 = recv3[2 * r, 8 * h : 8 * h + 8, :], recv3[2 * r + 1, 8 * h : 8 * h + 8, :]
            out[pl.ds(64 * h + r, 8, stride=8), :] = jnp.where(low, c0, pltpu.roll(c1, 64, 1))
            out[pl.ds(128 + 64 * h + r, 8, stride=8), :] = jnp.where(low, pltpu.roll(c0, 64, 1), c1)

    for dest in others:
        share(dest).wait_send()
        spread(send2, recv2, s2_sem, r2_sem, dest).wait_send()
        spread(send3, recv3, s3_sem, r3_sem, dest).wait_send()
    for buf, phase in ((src1, 0), (src2, 1)):
        for side in range(2):
            halo(buf, phase, side).wait_send()


def solution(mesh):
    n_tile = mesh.shape["tile"]
    f32, i32, bf16 = jnp.float32, jnp.int32, jnp.bfloat16
    anywhere = pl.BlockSpec(memory_space=pltpu.HBM)

    def on_device(tracers, courant, shear, offsets, seam_flips, kernel, coag_target):
        result = pl.pallas_call(
            functools.partial(body, n_tile),
            out_shape=jax.ShapeDtypeStruct((256, 128), f32),
            in_specs=[anywhere] * 4 + [pl.BlockSpec(memory_space=pltpu.SMEM)] + [anywhere] * 2,
            out_specs=pl.BlockSpec(memory_space=pltpu.VMEM),
            scratch_shapes=[
                pltpu.VMEM((256, 128), f32),
                pltpu.VMEM((24, 8), f32),
                pltpu.VMEM((24, 8), f32),
                pltpu.VMEM((24, 128), i32),
                pltpu.VMEM((32, 32), f32),
                pltpu.VMEM((32, 32), i32),
                pltpu.VMEM((24, 128), f32),
                pltpu.VMEM((2, 128), f32),
                pltpu.VMEM((TRC, 2, 128), f32),
                pltpu.VMEM((50, 8, 128), f32),
                pltpu.VMEM((16, 32, 128), f32),
                pltpu.VMEM((16, 32, 128), f32),
                pltpu.VMEM((TRC, 16, 128), f32),
                pltpu.VMEM((TRC, 16, 128), f32),
                pltpu.VMEM((BINS + 1, 16, 256), bf16),
                pltpu.VMEM((64, 128), f32),
                pltpu.VMEM((BINS + 1, 16, 128), f32),
                pltpu.VMEM((16, 128), f32),
                pltpu.VMEM((TRC, 16, 128), f32),
                pltpu.VMEM((TRC, 16, 128), f32),
                pltpu.SemaphoreType.DMA((6,)),
                pltpu.SemaphoreType.DMA((2, 2)),
                pltpu.SemaphoreType.DMA((2, 2)),
                pltpu.SemaphoreType.DMA((TRC,)),
                pltpu.SemaphoreType.DMA((TRC,)),
                pltpu.SemaphoreType.DMA((TRC,)),
                pltpu.SemaphoreType.DMA((TRC,)),
                pltpu.SemaphoreType.DMA((TRC,)),
                pltpu.SemaphoreType.DMA((TRC,)),
            ],
            compiler_params=pltpu.CompilerParams(
                collective_id=0, has_side_effects=True, vmem_limit_bytes=48 * 1024 * 1024
            ),
        )(
            tracers.reshape(256, 128), courant.reshape(24, 8), shear.reshape(24, 8),
            offsets.reshape(24, 128), seam_flips, kernel, coag_target,
        )
        return result.reshape(32, 4, 2, 128)

    return jax.shard_map(
        on_device,
        mesh=mesh,
        in_specs=(
            P("trc", "tile", None, None),
            P(None, "tile", None, "trc"),
            P(None, "tile", None, "trc"),
            P(None, "tile", None, None),
            P(),
            P(),
            P(),
        ),
        out_specs=P("trc", "tile", None, None),
        check_vma=False,
    )
```

```python
import functools

import jax
import jax.numpy as jnp
from jax import lax
from jax.experimental import pallas as pl
from jax.experimental.pallas import tpu as pltpu
from jax.sharding import PartitionSpec as P

BINS = 32
COMPS = 16
ITER = 3
TRC = 16
SIDE = 4
MESH = pl.DeviceIdType.MESH
EXACT = lax.Precision.HIGHEST


def taps(f, lower):
    p0 = -f * (f - 1.0) * (f - 2.0) / 6.0
    p1 = (f + 1.0) * (f - 1.0) * (f - 2.0) / 2.0
    p2 = -(f + 1.0) * f * (f - 2.0) / 2.0
    p3 = (f + 1.0) * f * (f - 1.0) / 6.0
    zero = jnp.zeros_like(f)
    return [
        jnp.where(lower, p0, zero),
        jnp.where(lower, p1, p0),
        jnp.where(lower, p2, p1),
        jnp.where(lower, p3, p2),
        jnp.where(lower, zero, p3),
    ]


def transport(src, wbuf, x):
    out = None
    for b in range(5):
        acc = [[None] * 4, [None] * 4]
        for a in range(5):
            for level in range(2):
                q = [src[2 * x + 2 * a + level, pl.ds(8 * g, 8), :] for g in range(4)]
                for l in range(2):
                    w = wbuf[(b * 5 + a) * 2 + level, pl.ds(2 * x + l, 1), :]
                    w = jnp.broadcast_to(w, (8, 128))
                    for g in range(4):
                        term = w * q[g]
                        acc[l][g] = term if acc[l][g] is None else acc[l][g] + term
        if b != 2:
            acc = [[pltpu.roll(v, (2 - b) % 128, 1) for v in row] for row in acc]
        out = acc if out is None else [[o + v for o, v in zip(r, s)] for r, s in zip(out, acc)]
    return out


def body(
    n_tile, tr, co, sh, of, fi, ke, ct, out,
    tin, cin, sin, oin, fl, kin, ctin, fpad, fsend, frecv, wbuf, src1, src2,
    send2, recv2, abuf, nbuf, tbuf, rbuf, send3, recv3,
    in_sem, hs_sem, hr_sem, fs_sem, fr_sem, s2_sem, r2_sem, s3_sem, r3_sem,
):
    tile, me = lax.axis_index("tile"), lax.axis_index("trc")
    x_me, z_me = me // SIDE, lax.rem(me, SIDE)
    prev = lax.rem(tile + n_tile - 1, n_tile)
    after = lax.rem(tile + 1, n_tile)

    loads = [
        pltpu.make_async_copy(s, d, in_sem.at[i])
        for i, (s, d) in enumerate(
            ((co, cin), (sh, sin), (tr, tin), (of, oin), (ke, kin), (ct, ctin), (fi, fl))
        )
    ]
    for load in loads:
        load.start()

    barrier = pltpu.get_barrier_semaphore()
    for k in range(1, TRC):
        pl.semaphore_signal(barrier, inc=1, device_id=(tile, lax.rem(me + k, TRC)), device_id_type=MESH)
    for t in (prev, after):
        pl.semaphore_signal(barrier, inc=1, device_id=(t, me), device_id_type=MESH)

    lane = lax.broadcasted_iota(jnp.int32, (8, 128), 1)
    sub = lax.broadcasted_iota(jnp.int32, (8, 128), 0)
    low = lane < 64

    fpad[...] = jnp.zeros_like(fpad)
    loads[0].wait()
    loads[1].wait()
    c, s = cin[...], sin[...]
    f = jnp.full(c.shape, 0.5, jnp.float32)
    for _ in range(ITER):
        f = jax.nn.sigmoid(c + s * (f - 0.5))
    fpad[:, 0:8] = f
    zero = jnp.zeros((8, 128), jnp.float32)
    rows = []
    for packed in (fpad[0:8] + pltpu.roll(fpad[8:16], 8, 1), fpad[16:24]):
        for bit in (1, 2, 4):
            packed = jnp.where(lax.rem(sub // bit, 2) == 1, pltpu.roll(packed, 128 - 16 * bit, 1), packed)
        packed = pltpu.roll(packed, me * 8, 1)
        rows.append(jnp.sum(packed, axis=0, keepdims=True))
    top, bottom = rows
    fsend[0:1, :] = top
    fsend[1:2, :] = bottom
    frecv[me, 0:1, :] = top
    frecv[me, 1:2, :] = bottom

    loads[2].wait()
    for r in range(8):
        for g in range(4):
            src1[4 + r, pl.ds(8 * g, 8), :] = tin[pl.ds(64 * g + r, 8, stride=8), :]

    pl.semaphore_wait(barrier, TRC + 1)

    def halo(buf, phase, side):
        return pltpu.make_async_remote_copy(
            src_ref=buf.at[pl.ds(4 + 4 * side, 4)],
            dst_ref=buf.at[pl.ds(12 - 12 * side, 4)],
            send_sem=hs_sem.at[phase, side],
            recv_sem=hr_sem.at[phase, side],
            device_id=((prev, after)[side], me),
            device_id_type=MESH,
        )

    def share(dest):
        return pltpu.make_async_remote_copy(
            src_ref=fsend, dst_ref=frecv.at[me], send_sem=fs_sem.at[dest], recv_sem=fr_sem.at[me],
            device_id=(tile, dest), device_id_type=MESH,
        )

    def spread(src, dst, s_sem, r_sem, dest):
        return pltpu.make_async_remote_copy(
            src_ref=src.at[dest], dst_ref=dst.at[me], send_sem=s_sem.at[dest], recv_sem=r_sem.at[me],
            device_id=(tile, dest), device_id_type=MESH,
        )

    def arrived(dst, r_sem, s_sem, source):
        return pltpu.make_async_remote_copy(
            src_ref=dst.at[source], dst_ref=dst.at[source], send_sem=s_sem.at[source],
            recv_sem=r_sem.at[source], device_id=(tile, source), device_id_type=MESH,
        )

    others = [lax.rem(me + k, TRC) for k in range(1, TRC)]
    for dest in others:
        share(dest).start()
    halo(src1, 0, 0).start()
    halo(src1, 0, 1).start()

    loads[4].wait()
    loads[5].wait()
    spot = lax.broadcasted_iota(jnp.int32, (32, 256), 1)
    j = lax.broadcasted_iota(jnp.int32, (32, 256), 0)
    at = lax.rem(j, 2) * 16 + j // 2
    rate = jnp.zeros((16, 256), jnp.float32)
    target = jnp.zeros((16, 256), jnp.float32)
    for p in range(2):
        place = (lax.rem(spot, 64) == at + 32 * p).astype(jnp.float32)
        rate += jnp.dot(kin[pl.ds(p, 16, stride=2), :], place, precision=EXACT, preferred_element_type=jnp.float32)
        target += jnp.dot(
            ctin[pl.ds(p, 16, stride=2), :].astype(jnp.float32), place, precision=EXACT,
            preferred_element_type=jnp.float32,
        )
    coarse = rate.astype(jnp.bfloat16).astype(jnp.float32)
    rate = jnp.where(lax.broadcasted_iota(jnp.int32, (16, 256), 1) < 128, coarse, rate - coarse)

    def fill(b, carry):
        hit = jnp.abs(target - b.astype(jnp.float32)) < 0.5
        abuf[b] = jnp.where(hit, rate, 0.0).astype(jnp.bfloat16)
        return carry

    lax.fori_loop(0, BINS, fill, 0)
    abuf[BINS] = rate.astype(jnp.bfloat16)

    loads[3].wait()
    for source in others:
        arrived(frecv, fr_sem, fs_sem, source).wait_recv()
    place = lax.rem(lane // 8 + 2 * sub, 16)
    spots = [place, lax.rem(place + 15, 16), place]
    frac = [zero, zero, zero]
    for source in range(TRC):
        rows = [jnp.broadcast_to(frecv[source, i : i + 1, :], (8, 128)) for i in (0, 0, 1)]
        frac = [jnp.where(spots[d] == source, rows[d], frac[d]) for d in range(3)]
    frac[1] = pltpu.roll(frac[1], 120, 1)
    weights = []
    for d in range(3):
        fd = pltpu.roll(frac[d], 0, 1, stride=16, stride_axis=0)
        weights.append(taps(fd, oin[8 * d : 8 * d + 8, :] == -1))
    cross, levels, along = weights
    upper = lax.rem(sub, 2) == 1
    level0 = levels[0] + levels[1] + jnp.where(upper, zero, levels[2])
    level1 = levels[3] + levels[4] + jnp.where(upper, levels[2], zero)
    for a in range(5):
        for level, lw in enumerate((level0, level1)):
            pair = cross[a] * lw
            for b in range(5):
                w = pair * along[b]
                if b != 2:
                    w = pltpu.roll(w, (b - 2) % 128, 1)
                wbuf[(b * 5 + a) * 2 + level] = w

    loads[6].wait()
    flags = (fl[tile], fl[after])
    mirror = 127 - lane

    def turn(buf, side):
        turned = jnp.full((8, 128), flags[side], jnp.int32) == 1

        for i in range(4):
            for g in range(4):
                at = (12 * side + i, pl.ds(8 * g, 8), slice(None))
                v = buf[at]
                buf[at] = jnp.where(turned, jnp.take_along_axis(v, mirror, axis=1), v)

    def rims(buf, phase):
        for side in (1, 0):
            halo(buf, phase, side).wait_recv()
            turn(buf, 1 - side)

    rims(src1, 0)

    def first(x, carry):
        moved = transport(src1, wbuf, x)
        for l in range(2):
            for g in range(4):
                src2[4 + 2 * x + l, pl.ds(8 * g, 8), :] = moved[l][g]
        return carry

    lax.fori_loop(0, 2, first, 0)
    halo(src2, 1, 0).start()
    lax.fori_loop(2, 4, first, 0)
    halo(src2, 1, 1).start()
    rims(src2, 1)

    def plane(k):
        return lax.rem(x_me + 6 - k + 3 * (k // 2) + 2 * (k // 3), SIDE)

    def second(k, carry):
        x = plane(k)
        moved = transport(src2, wbuf, x)
        for l in range(2):
            for g in range(2):
                even, odd = moved[l][g], moved[l][2 + g]
                at = pl.ds(8 * g, 8)
                send2[4 * x + 2 * l, at, :] = jnp.where(low, even, pltpu.roll(odd, 64, 1))
                send2[4 * x + 2 * l + 1, at, :] = jnp.where(low, pltpu.roll(even, 64, 1), odd)
        for i in (2, 1, 3):
            spread(send2, recv2, s2_sem, r2_sem, 4 * x + lax.rem(z_me + i, SIDE)).start()

        @pl.when(k < SIDE - 1)
        def _():
            spread(send2, recv2, s2_sem, r2_sem, 4 * x + z_me).start()

        return carry

    lax.fori_loop(0, SIDE, second, 0)
    recv2[me] = send2[me]
    for source in others:
        arrived(recv2, r2_sem, s2_sem, source).wait_recv()

    number = jnp.sum(jnp.abs(recv2[...]), axis=1)
    low16 = lax.broadcasted_iota(jnp.int32, (16, 128), 1) < 64
    other = pltpu.roll(number, 64, 1)
    none = jnp.zeros_like(number)
    nums = jnp.concatenate(
        [
            jnp.where(low16, number, none),
            jnp.where(low16, other, none),
            jnp.where(low16, none, other),
            jnp.where(low16, none, number),
        ],
        axis=0,
    )
    coarse = nums.astype(jnp.bfloat16)
    fine = (nums - coarse.astype(jnp.float32)).astype(jnp.bfloat16)
    nums = jnp.concatenate([coarse, fine, coarse, fine], axis=0)
    rates = jnp.dot(
        abuf[...].reshape((BINS + 1) * 16, 256), nums, preferred_element_type=jnp.float32
    )
    tbuf[...] = rates.reshape(BINS + 1, 16, 128)
    rbuf[...] = 1.0 / (1.0 + tbuf[BINS])

    def gain(k, carry):
        x = plane(k)
        acc = [[None] * 2 for _ in range(8)]
        for i in range(TRC):
            m = [recv2[i, 0:8, :], recv2[i, 8:16, :]]
            for b in range(8):
                t = jnp.broadcast_to(tbuf[8 * x + b, i : i + 1, :], (8, 128))
                for h in range(2):
                    term = t * m[h]
                    acc[b][h] = term if acc[b][h] is None else acc[b][h] + term
        for z in range(SIDE):
            g = 4 * x + z
            rec = jnp.broadcast_to(rbuf[pl.ds(g, 1), :], (8, 128))
            for h in range(2):
                even, odd = acc[2 * z][h], acc[2 * z + 1][h]
                gained = jnp.where(low, even, odd) + pltpu.roll(jnp.where(low, odd, even), 64, 1)
                send3[g, 8 * h : 8 * h + 8, :] = (recv2[g, 8 * h : 8 * h + 8, :] + gained) * rec
        for z in range(SIDE):

            @pl.when(4 * x + z != me)
            def _(z=z):
                spread(send3, recv3, s3_sem, r3_sem, 4 * x + z).start()

        return carry

    lax.fori_loop(0, SIDE, gain, 0)
    recv3[me] = send3[me]
    for source in others:
        arrived(recv3, r3_sem, s3_sem, source).wait_recv()
    for r in range(8):
        for h in range(2):
            c0, c1 = recv3[2 * r, 8 * h : 8 * h + 8, :], recv3[2 * r + 1, 8 * h : 8 * h + 8, :]
            out[pl.ds(64 * h + r, 8, stride=8), :] = jnp.where(low, c0, pltpu.roll(c1, 64, 1))
            out[pl.ds(128 + 64 * h + r, 8, stride=8), :] = jnp.where(low, pltpu.roll(c0, 64, 1), c1)

    for dest in others:
        share(dest).wait_send()
        spread(send2, recv2, s2_sem, r2_sem, dest).wait_send()
        spread(send3, recv3, s3_sem, r3_sem, dest).wait_send()
    for buf, phase in ((src1, 0), (src2, 1)):
        for side in range(2):
            halo(buf, phase, side).wait_send()


def solution(mesh):
    n_tile = mesh.shape["tile"]
    f32, i32, bf16 = jnp.float32, jnp.int32, jnp.bfloat16
    anywhere = pl.BlockSpec(memory_space=pltpu.HBM)

    def on_device(tracers, courant, shear, offsets, seam_flips, kernel, coag_target):
        result = pl.pallas_call(
            functools.partial(body, n_tile),
            out_shape=jax.ShapeDtypeStruct((256, 128), f32),
            in_specs=[anywhere] * 7,
            out_specs=pl.BlockSpec(memory_space=pltpu.VMEM),
            scratch_shapes=[
                pltpu.VMEM((256, 128), f32),
                pltpu.VMEM((24, 8), f32),
                pltpu.VMEM((24, 8), f32),
                pltpu.VMEM((24, 128), i32),
                pltpu.SMEM((32,), i32),
                pltpu.VMEM((32, 32), f32),
                pltpu.VMEM((32, 32), i32),
                pltpu.VMEM((24, 128), f32),
                pltpu.VMEM((2, 128), f32),
                pltpu.VMEM((TRC, 2, 128), f32),
                pltpu.VMEM((50, 8, 128), f32),
                pltpu.VMEM((16, 32, 128), f32),
                pltpu.VMEM((16, 32, 128), f32),
                pltpu.VMEM((TRC, 16, 128), f32),
                pltpu.VMEM((TRC, 16, 128), f32),
                pltpu.VMEM((BINS + 1, 16, 256), bf16),
                pltpu.VMEM((64, 128), f32),
                pltpu.VMEM((BINS + 1, 16, 128), f32),
                pltpu.VMEM((16, 128), f32),
                pltpu.VMEM((TRC, 16, 128), f32),
                pltpu.VMEM((TRC, 16, 128), f32),
                pltpu.SemaphoreType.DMA((7,)),
                pltpu.SemaphoreType.DMA((2, 2)),
                pltpu.SemaphoreType.DMA((2, 2)),
                pltpu.SemaphoreType.DMA((TRC,)),
                pltpu.SemaphoreType.DMA((TRC,)),
                pltpu.SemaphoreType.DMA((TRC,)),
                pltpu.SemaphoreType.DMA((TRC,)),
                pltpu.SemaphoreType.DMA((TRC,)),
                pltpu.SemaphoreType.DMA((TRC,)),
            ],
            compiler_params=pltpu.CompilerParams(
                collective_id=0, has_side_effects=True, vmem_limit_bytes=48 * 1024 * 1024
            ),
        )(
            *(
                pltpu.with_memory_space_constraint(v, pltpu.HBM)
                for v in (
                    tracers.reshape(256, 128), courant.reshape(24, 8), shear.reshape(24, 8),
                    offsets.reshape(24, 128), seam_flips, kernel, coag_target,
                )
            ),
        )
        return result.reshape(32, 4, 2, 128)

    return jax.shard_map(
        on_device,
        mesh=mesh,
        in_specs=(
            P("trc", "tile", None, None),
            P(None, "tile", None, "trc"),
            P(None, "tile", None, "trc"),
            P(None, "tile", None, None),
            P(),
            P(),
            P(),
        ),
        out_specs=P("trc", "tile", None, None),
        check_vma=False,
    )
```

```python
import functools

import jax
import jax.numpy as jnp
from jax import lax
from jax.experimental import pallas as pl
from jax.experimental.pallas import tpu as pltpu
from jax.sharding import PartitionSpec as P

BINS = 32
COMPS = 16
ITER = 3
TRC = 16
SIDE = 4
MESH = pl.DeviceIdType.MESH
EXACT = lax.Precision.HIGHEST


def taps(f, lower):
    p0 = -f * (f - 1.0) * (f - 2.0) / 6.0
    p1 = (f + 1.0) * (f - 1.0) * (f - 2.0) / 2.0
    p2 = -(f + 1.0) * f * (f - 2.0) / 2.0
    p3 = (f + 1.0) * f * (f - 1.0) / 6.0
    zero = jnp.zeros_like(f)
    return [
        jnp.where(lower, p0, zero),
        jnp.where(lower, p1, p0),
        jnp.where(lower, p2, p1),
        jnp.where(lower, p3, p2),
        jnp.where(lower, zero, p3),
    ]


def transport(src, wbuf, x):
    out = None
    for b in range(5):
        acc = [[None] * 4, [None] * 4]
        for a in range(5):
            for level in range(2):
                q = [src[2 * x + 2 * a + level, pl.ds(8 * g, 8), :] for g in range(4)]
                for l in range(2):
                    w = wbuf[(b * 5 + a) * 2 + level, pl.ds(2 * x + l, 1), :]
                    w = jnp.broadcast_to(w, (8, 128))
                    for g in range(4):
                        term = w * q[g]
                        acc[l][g] = term if acc[l][g] is None else acc[l][g] + term
        if b != 2:
            acc = [[pltpu.roll(v, (2 - b) % 128, 1) for v in row] for row in acc]
        out = acc if out is None else [[o + v for o, v in zip(r, s)] for r, s in zip(out, acc)]
    return out


def body(
    n_tile, tr, co, sh, of, fi, ke, ct, out,
    tin, cin, sin, oin, fl, kin, ctin, fpad, fsend, frecv, wbuf, src1, src2,
    send2, recv2, abuf, nbuf, tbuf, rbuf, send3, recv3,
    in_sem, hs_sem, hr_sem, fs_sem, fr_sem, s2_sem, r2_sem, s3_sem, r3_sem,
):
    tile, me = lax.axis_index("tile"), lax.axis_index("trc")
    x_me, z_me = me // SIDE, lax.rem(me, SIDE)
    prev = lax.rem(tile + n_tile - 1, n_tile)
    after = lax.rem(tile + 1, n_tile)

    quad = lax.rem(tile, 4)
    side_far = lax.rem(quad, 2)
    partner = tile + 2 - 4 * (quad // 2)

    def plane(k):
        return lax.rem(x_me + 6 - k + 3 * (k // 2) + 2 * (k // 3), SIDE)

    others = [4 * plane(k) + lax.rem(z_me + i, SIDE) for k in range(SIDE) for i in (2, 1, 3, 0)][:-1]
    barrier = pltpu.get_barrier_semaphore()
    for dest in others:
        pl.semaphore_signal(barrier, inc=1, device_id=(tile, dest), device_id_type=MESH)
    for t in (prev, after):
        pl.semaphore_signal(barrier, inc=1, device_id=(t, me), device_id_type=MESH)

    loads = [
        pltpu.make_async_copy(s, d, in_sem.at[i])
        for i, (s, d) in enumerate(
            ((co, cin), (sh, sin), (tr, tin), (of, oin), (ke, kin), (ct, ctin), (fi, fl))
        )
    ]
    for load in loads:
        load.start()
    for k in range(TRC):
        dest = lax.rem(me + k, TRC)
        pl.semaphore_signal(barrier, inc=1, device_id=(partner, dest), device_id_type=MESH)

    lane = lax.broadcasted_iota(jnp.int32, (8, 128), 1)
    sub = lax.broadcasted_iota(jnp.int32, (8, 128), 0)
    low = lane < 64

    fpad[...] = jnp.zeros_like(fpad)
    loads[0].wait()
    loads[1].wait()
    c, s = cin[...], sin[...]
    f = jnp.full(c.shape, 0.5, jnp.float32)
    for _ in range(ITER):
        f = jax.nn.sigmoid(c + s * (f - 0.5))
    fpad[:, 0:8] = f
    zero = jnp.zeros((8, 128), jnp.float32)
    rows = []
    for packed in (fpad[0:8] + pltpu.roll(fpad[8:16], 8, 1), fpad[16:24]):
        for bit in (1, 2, 4):
            packed = jnp.where(lax.rem(sub // bit, 2) == 1, pltpu.roll(packed, 128 - 16 * bit, 1), packed)
        packed = pltpu.roll(packed, me * 8, 1)
        rows.append(jnp.sum(packed, axis=0, keepdims=True))
    top, bottom = rows
    fsend[0:1, :] = top
    fsend[1:2, :] = bottom
    frecv[me, 0:1, :] = top
    frecv[me, 1:2, :] = bottom

    loads[2].wait()
    for r in range(8):
        for g in range(4):
            src1[4 + r, pl.ds(8 * g, 8), :] = tin[pl.ds(64 * g + r, 8, stride=8), :]

    pl.semaphore_wait(barrier, 2 * TRC + 1)

    def halo(side):
        return pltpu.make_async_remote_copy(
            src_ref=src1.at[pl.ds(4 + 4 * side, 4)],
            dst_ref=src1.at[pl.ds(12 - 12 * side, 4)],
            send_sem=hs_sem.at[0, side],
            recv_sem=hr_sem.at[0, side],
            device_id=((prev, after)[side], me),
            device_id_type=MESH,
        )

    def moved_halo(side, i):
        return pltpu.make_async_remote_copy(
            src_ref=src2.at[pl.ds(4 + 4 * side + 2 * i, 2)],
            dst_ref=src2.at[pl.ds(12 - 12 * side + 2 * i, 2)],
            send_sem=hs_sem.at[1 + i, side],
            recv_sem=hr_sem.at[1 + i, side],
            device_id=(lax.rem(tile + n_tile - 1 + 2 * side, n_tile), me),
            device_id_type=MESH,
        )

    def share(dest):
        return pltpu.make_async_remote_copy(
            src_ref=fsend, dst_ref=frecv.at[me], send_sem=fs_sem.at[dest], recv_sem=fr_sem.at[me],
            device_id=(tile, dest), device_id_type=MESH,
        )

    def spread(src, dst, s_sem, r_sem, dest):
        return pltpu.make_async_remote_copy(
            src_ref=src.at[dest], dst_ref=dst.at[me], send_sem=s_sem.at[dest], recv_sem=r_sem.at[me],
            device_id=(partner, dest), device_id_type=MESH,
        )

    def arrived(dst, r_sem, s_sem, source):
        return pltpu.make_async_remote_copy(
            src_ref=dst.at[source], dst_ref=dst.at[source], send_sem=s_sem.at[source],
            recv_sem=r_sem.at[source], device_id=(tile, source), device_id_type=MESH,
        )

    for dest in others:
        share(dest).start()
    halo(0).start()
    halo(1).start()

    loads[4].wait()
    loads[5].wait()
    spot = lax.broadcasted_iota(jnp.int32, (32, 256), 1)
    j = lax.broadcasted_iota(jnp.int32, (32, 256), 0)
    at = lax.rem(j, 2) * 16 + j // 2
    rate = jnp.zeros((16, 256), jnp.float32)
    target = jnp.zeros((16, 256), jnp.float32)
    for p in range(2):
        place = (lax.rem(spot, 64) == at + 32 * p).astype(jnp.float32)
        rate += jnp.dot(kin[pl.ds(p, 16, stride=2), :], place, precision=EXACT, preferred_element_type=jnp.float32)
        target += jnp.dot(
            ctin[pl.ds(p, 16, stride=2), :].astype(jnp.float32), place, precision=EXACT,
            preferred_element_type=jnp.float32,
        )
    coarse = rate.astype(jnp.bfloat16).astype(jnp.float32)
    rate = jnp.where(lax.broadcasted_iota(jnp.int32, (16, 256), 1) < 128, coarse, rate - coarse)

    def fill(b, carry):
        hit = jnp.abs(target - b.astype(jnp.float32)) < 0.5
        abuf[b] = jnp.where(hit, rate, 0.0).astype(jnp.bfloat16)
        return carry

    lax.fori_loop(0, BINS, fill, 0)
    abuf[BINS] = rate.astype(jnp.bfloat16)

    mirror = 127 - lane
    loads[6].wait()

    def turn(buf, side):
        turned = jnp.full((8, 128), fl[lax.rem(tile + side, n_tile)], jnp.int32) == 1
        for i in range(4):
            for g in range(4):
                at = (12 * side + i, pl.ds(8 * g, 8), slice(None))
                v = buf[at]
                buf[at] = jnp.where(turned, jnp.take_along_axis(v, mirror, axis=1), v)

    for side in range(2):
        halo(1 - side).wait_recv()
        turn(src1, side)

    loads[3].wait()
    for source in others:
        arrived(frecv, fr_sem, fs_sem, source).wait_recv()
    place = lax.rem(lane // 8 + 2 * sub, 16)
    spots = [place, lax.rem(place + 15, 16), place]
    frac = [zero, zero, zero]
    for source in range(TRC):
        rows = [jnp.broadcast_to(frecv[source, i : i + 1, :], (8, 128)) for i in (0, 0, 1)]
        frac = [jnp.where(spots[d] == source, rows[d], frac[d]) for d in range(3)]
    frac[1] = pltpu.roll(frac[1], 120, 1)
    weights = []
    for d in range(3):
        fd = pltpu.roll(frac[d], 0, 1, stride=16, stride_axis=0)
        weights.append(taps(fd, oin[8 * d : 8 * d + 8, :] == -1))
    cross, levels, along = weights
    upper = lax.rem(sub, 2) == 1
    level0 = levels[0] + levels[1] + jnp.where(upper, zero, levels[2])
    level1 = levels[3] + levels[4] + jnp.where(upper, levels[2], zero)
    for a in range(5):
        for level, lw in enumerate((level0, level1)):
            pair = cross[a] * lw
            for b in range(5):
                w = pair * along[b]
                if b != 2:
                    w = pltpu.roll(w, (b - 2) % 128, 1)
                wbuf[(b * 5 + a) * 2 + level] = w

    def first(k, carry):
        side = lax.rem(side_far + k // 2, 2)
        x = 2 * side + lax.rem(k, 2)
        moved = transport(src1, wbuf, x)
        for l in range(2):
            for g in range(4):
                src2[4 + 2 * x + l, pl.ds(8 * g, 8), :] = moved[l][g]
        moved_halo(side, lax.rem(k, 2)).start()
        return carry

    lax.fori_loop(0, 4, first, 0)

    def rim(side):
        for i in range(2):
            moved_halo(1 - side, i).wait_recv()
        turn(src2, side)

    def second(k, carry):
        pair = 2 * lax.rem(1 - side_far + k // 2, 2)
        near = lax.rem(x_me + 5 - pair, SIDE) // 2
        x = pair + lax.rem(1 - near + k, 2)
        moved = transport(src2, wbuf, x)
        for l in range(2):
            for g in range(2):
                even, odd = moved[l][g], moved[l][2 + g]
                at = pl.ds(8 * g, 8)
                send2[4 * x + 2 * l, at, :] = jnp.where(low, even, pltpu.roll(odd, 64, 1))
                send2[4 * x + 2 * l + 1, at, :] = jnp.where(low, pltpu.roll(even, 64, 1), odd)
        for i in range(SIDE):
            spread(send2, recv2, s2_sem, r2_sem, 4 * x + zs[i]).start()
        return carry

    zs = [lax.rem(z_me + 1 + quad // 2 + i, SIDE) for i in range(SIDE)]
    rim(1 - side_far)
    lax.fori_loop(0, 2, second, 0)
    rim(side_far)
    lax.fori_loop(2, 4, second, 0)

    sources = [4 * plane(k) + lax.rem(z_me + quad // 2 + 3 + i, SIDE) for k in (3, 2, 1, 0) for i in range(SIDE)]
    for source in sources:
        arrived(recv2, r2_sem, s2_sem, source).wait_recv()
        nbuf[pl.ds(source, 1), :] = jnp.sum(jnp.abs(recv2[source]), axis=0, keepdims=True)
    number = nbuf[...]
    low16 = lax.broadcasted_iota(jnp.int32, (16, 128), 1) < 64
    other = pltpu.roll(number, 64, 1)
    none = jnp.zeros_like(number)
    nums = jnp.concatenate(
        [
            jnp.where(low16, number, none),
            jnp.where(low16, other, none),
            jnp.where(low16, none, other),
            jnp.where(low16, none, number),
        ],
        axis=0,
    )
    coarse = nums.astype(jnp.bfloat16)
    fine = (nums - coarse.astype(jnp.float32)).astype(jnp.bfloat16)
    nums = jnp.concatenate([coarse, fine, coarse, fine], axis=0)
    rates = jnp.dot(
        abuf[...].reshape((BINS + 1) * 16, 256), nums, preferred_element_type=jnp.float32
    )
    tbuf[...] = rates.reshape(BINS + 1, 16, 128)
    rbuf[...] = 1.0 / (1.0 + tbuf[BINS])

    def gain(k, carry):
        x = plane(k)
        acc = [[None] * 2 for _ in range(8)]
        for i in range(TRC):
            m = [recv2[i, 0:8, :], recv2[i, 8:16, :]]
            for b in range(8):
                t = jnp.broadcast_to(tbuf[8 * x + b, i : i + 1, :], (8, 128))
                for h in range(2):
                    term = t * m[h]
                    acc[b][h] = term if acc[b][h] is None else acc[b][h] + term
        for z in range(SIDE):
            g = 4 * x + z
            rec = jnp.broadcast_to(rbuf[pl.ds(g, 1), :], (8, 128))
            for h in range(2):
                even, odd = acc[2 * z][h], acc[2 * z + 1][h]
                gained = jnp.where(low, even, odd) + pltpu.roll(jnp.where(low, odd, even), 64, 1)
                send3[g, 8 * h : 8 * h + 8, :] = (recv2[g, 8 * h : 8 * h + 8, :] + gained) * rec
        for i in range(SIDE):
            spread(send3, recv3, s3_sem, r3_sem, 4 * x + zs[i]).start()
        return carry

    lax.fori_loop(0, SIDE, gain, 0)
    for k in (3, 2, 1, 0):
        x = plane(k)
        for z in range(SIDE):
            arrived(recv3, r3_sem, s3_sem, 4 * x + z).wait_recv()
        for i in range(2):
            r = 2 * x + i
            for h in range(2):
                c0, c1 = recv3[2 * r, 8 * h : 8 * h + 8, :], recv3[2 * r + 1, 8 * h : 8 * h + 8, :]
                out[pl.ds(64 * h + r, 8, stride=8), :] = jnp.where(low, c0, pltpu.roll(c1, 64, 1))
                out[pl.ds(128 + 64 * h + r, 8, stride=8), :] = jnp.where(low, pltpu.roll(c0, 64, 1), c1)

    for dest in others:
        share(dest).wait_send()
    for dest in range(TRC):
        spread(send2, recv2, s2_sem, r2_sem, dest).wait_send()
        spread(send3, recv3, s3_sem, r3_sem, dest).wait_send()
    for side in range(2):
        halo(side).wait_send()
        for i in range(2):
            moved_halo(side, i).wait_send()


def solution(mesh):
    n_tile = mesh.shape["tile"]
    f32, i32, bf16 = jnp.float32, jnp.int32, jnp.bfloat16
    anywhere = pl.BlockSpec(memory_space=pltpu.HBM)

    def on_device(tracers, courant, shear, offsets, seam_flips, kernel, coag_target):
        result = pl.pallas_call(
            functools.partial(body, n_tile),
            out_shape=jax.ShapeDtypeStruct((256, 128), f32),
            in_specs=[anywhere] * 7,
            out_specs=pl.BlockSpec(memory_space=pltpu.VMEM),
            scratch_shapes=[
                pltpu.VMEM((256, 128), f32),
                pltpu.VMEM((24, 8), f32),
                pltpu.VMEM((24, 8), f32),
                pltpu.VMEM((24, 128), i32),
                pltpu.SMEM((32,), i32),
                pltpu.VMEM((32, 32), f32),
                pltpu.VMEM((32, 32), i32),
                pltpu.VMEM((24, 128), f32),
                pltpu.VMEM((2, 128), f32),
                pltpu.VMEM((TRC, 2, 128), f32),
                pltpu.VMEM((50, 8, 128), f32),
                pltpu.VMEM((16, 32, 128), f32),
                pltpu.VMEM((16, 32, 128), f32),
                pltpu.VMEM((TRC, 16, 128), f32),
                pltpu.VMEM((TRC, 16, 128), f32),
                pltpu.VMEM((BINS + 1, 16, 256), bf16),
                pltpu.VMEM((16, 128), f32),
                pltpu.VMEM((BINS + 1, 16, 128), f32),
                pltpu.VMEM((16, 128), f32),
                pltpu.VMEM((TRC, 16, 128), f32),
                pltpu.VMEM((TRC, 16, 128), f32),
                pltpu.SemaphoreType.DMA((7,)),
                pltpu.SemaphoreType.DMA((3, 2)),
                pltpu.SemaphoreType.DMA((3, 2)),
                pltpu.SemaphoreType.DMA((TRC,)),
                pltpu.SemaphoreType.DMA((TRC,)),
                pltpu.SemaphoreType.DMA((TRC,)),
                pltpu.SemaphoreType.DMA((TRC,)),
                pltpu.SemaphoreType.DMA((TRC,)),
                pltpu.SemaphoreType.DMA((TRC,)),
            ],
            compiler_params=pltpu.CompilerParams(
                collective_id=0, has_side_effects=True, vmem_limit_bytes=48 * 1024 * 1024
            ),
        )(
            *(
                pltpu.with_memory_space_constraint(v, pltpu.HBM)
                for v in (
                    tracers.reshape(256, 128), courant.reshape(24, 8), shear.reshape(24, 8),
                    offsets.reshape(24, 128), seam_flips, kernel, coag_target,
                )
            ),
        )
        return result.reshape(32, 4, 2, 128)

    return jax.shard_map(
        on_device,
        mesh=mesh,
        in_specs=(
            P("trc", "tile", None, None),
            P(None, "tile", None, "trc"),
            P(None, "tile", None, "trc"),
            P(None, "tile", None, None),
            P(),
            P(),
            P(),
        ),
        out_specs=P("trc", "tile", None, None),
        check_vma=False,
    )
```

```python
import functools

import jax
import jax.numpy as jnp
from jax import lax
from jax.experimental import pallas as pl
from jax.experimental.pallas import tpu as pltpu
from jax.sharding import PartitionSpec as P

BINS = 32
COMPS = 16
ITER = 3
TRC = 16
SIDE = 4
MESH = pl.DeviceIdType.MESH
EXACT = lax.Precision.HIGHEST


def taps(f, lower):
    p0 = -f * (f - 1.0) * (f - 2.0) / 6.0
    p1 = (f + 1.0) * (f - 1.0) * (f - 2.0) / 2.0
    p2 = -(f + 1.0) * f * (f - 2.0) / 2.0
    p3 = (f + 1.0) * f * (f - 1.0) / 6.0
    zero = jnp.zeros_like(f)
    return [
        jnp.where(lower, p0, zero),
        jnp.where(lower, p1, p0),
        jnp.where(lower, p2, p1),
        jnp.where(lower, p3, p2),
        jnp.where(lower, zero, p3),
    ]


def transport(src, wbuf, x, steps=range(5), out=None):
    for b in range(5):
        acc = [[None] * 4, [None] * 4]
        for a in steps:
            for level in range(2):
                q = [src[2 * x + 2 * a + level, pl.ds(8 * g, 8), :] for g in range(4)]
                for l in range(2):
                    w = wbuf[(b * 5 + a) * 2 + level, pl.ds(2 * x + l, 1), :]
                    w = jnp.broadcast_to(w, (8, 128))
                    for g in range(4):
                        term = w * q[g]
                        acc[l][g] = term if acc[l][g] is None else acc[l][g] + term
        if b != 2:
            acc = [[pltpu.roll(v, (2 - b) % 128, 1) for v in row] for row in acc]
        out = acc if out is None else [[o + v for o, v in zip(r, s)] for r, s in zip(out, acc)]
    return out


def body(
    n_tile, tr, co, sh, of, fi, ke, ct, out,
    tin, cin, sin, oin, fl, kin, ctin, fpad, fsend, frecv, wbuf, src1, src2, part,
    send2, recv2, abuf, nbuf, tbuf, rbuf, send3, recv3,
    in_sem, hs_sem, hr_sem, fs_sem, fr_sem, known_sem, s2_sem, r2_sem, s3_sem, r3_sem,
):
    tile, me = lax.axis_index("tile"), lax.axis_index("trc")
    x_me, z_me = me // SIDE, lax.rem(me, SIDE)
    prev = lax.rem(tile + n_tile - 1, n_tile)
    after = lax.rem(tile + 1, n_tile)

    quad = lax.rem(tile, 4)
    side_far = lax.rem(quad, 2)
    partner = tile + 2 - 4 * (quad // 2)

    def plane(k):
        return lax.rem(x_me + 6 - k + 3 * (k // 2) + 2 * (k // 3), SIDE)

    others = [4 * plane(k) + lax.rem(z_me + i, SIDE) for k in range(SIDE) for i in (2, 1, 3, 0)][:-1]
    barrier = pltpu.get_barrier_semaphore()
    for dest in others:
        pl.semaphore_signal(barrier, inc=1, device_id=(tile, dest), device_id_type=MESH)
    for t in (prev, after):
        pl.semaphore_signal(barrier, inc=1, device_id=(t, me), device_id_type=MESH)

    loads = [
        pltpu.make_async_copy(s, d, in_sem.at[i])
        for i, (s, d) in enumerate(
            ((co, cin), (sh, sin), (tr, tin), (of, oin), (ke, kin), (ct, ctin), (fi, fl))
        )
    ]
    for load in loads:
        load.start()

    lane = lax.broadcasted_iota(jnp.int32, (8, 128), 1)
    sub = lax.broadcasted_iota(jnp.int32, (8, 128), 0)
    low = lane < 64

    fpad[...] = jnp.zeros_like(fpad)
    loads[0].wait()
    loads[1].wait()
    c, s = cin[...], sin[...]
    f = jnp.full(c.shape, 0.5, jnp.float32)
    for _ in range(ITER):
        f = jax.nn.sigmoid(c + s * (f - 0.5))
    fpad[:, 0:8] = f
    zero = jnp.zeros((8, 128), jnp.float32)
    rows = []
    for packed in (fpad[0:8] + pltpu.roll(fpad[8:16], 8, 1), fpad[16:24]):
        for bit in (1, 2, 4):
            packed = jnp.where(lax.rem(sub // bit, 2) == 1, pltpu.roll(packed, 128 - 16 * bit, 1), packed)
        packed = pltpu.roll(packed, me * 8, 1)
        rows.append(jnp.sum(packed, axis=0, keepdims=True))
    top, bottom = rows
    fsend[0:1, :] = top
    fsend[1:2, :] = bottom
    frecv[me, 0:1, :] = top
    frecv[me, 1:2, :] = bottom

    loads[2].wait()
    for r in range(8):
        for g in range(4):
            src1[4 + r, pl.ds(8 * g, 8), :] = tin[pl.ds(64 * g + r, 8, stride=8), :]

    pl.semaphore_wait(barrier, TRC + 1)

    def halo(side):
        return pltpu.make_async_remote_copy(
            src_ref=src1.at[pl.ds(4 + 4 * side, 4)],
            dst_ref=src1.at[pl.ds(12 - 12 * side, 4)],
            send_sem=hs_sem.at[0, side],
            recv_sem=hr_sem.at[0, side],
            device_id=((prev, after)[side], me),
            device_id_type=MESH,
        )

    def moved_halo(side, i):
        return pltpu.make_async_remote_copy(
            src_ref=src2.at[pl.ds(4 + 4 * side + 2 * i, 2)],
            dst_ref=src2.at[pl.ds(12 - 12 * side + 2 * i, 2)],
            send_sem=hs_sem.at[1 + i, side],
            recv_sem=hr_sem.at[1 + i, side],
            device_id=(lax.rem(tile + n_tile - 1 + 2 * side, n_tile), me),
            device_id_type=MESH,
        )

    def share(dest):
        return pltpu.make_async_remote_copy(
            src_ref=fsend, dst_ref=frecv.at[me], send_sem=fs_sem.at[dest], recv_sem=fr_sem.at[me],
            device_id=(tile, dest), device_id_type=MESH,
        )

    def spread(src, dst, s_sem, r_sem, dest):
        return pltpu.make_async_remote_copy(
            src_ref=src.at[dest], dst_ref=dst.at[me], send_sem=s_sem.at[dest], recv_sem=r_sem.at[me],
            device_id=(partner, dest), device_id_type=MESH,
        )

    def arrived(dst, r_sem, s_sem, source):
        return pltpu.make_async_remote_copy(
            src_ref=dst.at[source], dst_ref=dst.at[source], send_sem=s_sem.at[source],
            recv_sem=r_sem.at[source], device_id=(tile, source), device_id_type=MESH,
        )

    for z in (3, 2, 1, 0):
        for i in (2, 1, 3, 0):
            dest = 4 * lax.rem(x_me + i, SIDE) + z

            @pl.when(dest != me)
            def _(dest=dest):
                share(dest).start()

    halo(0).start()
    halo(1).start()

    loads[4].wait()
    loads[5].wait()
    spot = lax.broadcasted_iota(jnp.int32, (32, 256), 1)
    j = lax.broadcasted_iota(jnp.int32, (32, 256), 0)
    at = lax.rem(j, 2) * 16 + j // 2
    rate = jnp.zeros((16, 256), jnp.float32)
    target = jnp.zeros((16, 256), jnp.float32)
    for p in range(2):
        place = (lax.rem(spot, 64) == at + 32 * p).astype(jnp.float32)
        rate += jnp.dot(kin[pl.ds(p, 16, stride=2), :], place, precision=EXACT, preferred_element_type=jnp.float32)
        target += jnp.dot(
            ctin[pl.ds(p, 16, stride=2), :].astype(jnp.float32), place, precision=EXACT,
            preferred_element_type=jnp.float32,
        )
    coarse = rate.astype(jnp.bfloat16).astype(jnp.float32)
    rate = jnp.where(lax.broadcasted_iota(jnp.int32, (16, 256), 1) < 128, coarse, rate - coarse)

    def fill(b, carry):
        hit = jnp.abs(target - b.astype(jnp.float32)) < 0.5
        abuf[1 + 8 * (lax.rem(b, 8) // 2) + 2 * (b // 8) + lax.rem(b, 2)] = jnp.where(hit, rate, 0.0).astype(jnp.bfloat16)
        return carry

    lax.fori_loop(0, BINS, fill, 0)
    abuf[0] = rate.astype(jnp.bfloat16)

    mirror = 127 - lane
    loads[6].wait()

    def turn(buf, side):
        turned = jnp.full((8, 128), fl[lax.rem(tile + side, n_tile)], jnp.int32) == 1
        for i in range(4):
            for g in range(4):
                at = (12 * side + i, pl.ds(8 * g, 8), slice(None))
                v = buf[at]
                buf[at] = jnp.where(turned, jnp.take_along_axis(v, mirror, axis=1), v)

    for side in range(2):
        halo(1 - side).wait_recv()
        turn(src1, side)

    loads[3].wait()
    for source in others:
        arrived(frecv, fr_sem, fs_sem, source).wait_recv()

    inner = (quad + 1) // 2 == 1

    @pl.when(inner)
    def _():
        pl.semaphore_signal(
            known_sem, inc=1, device_id=(lax.rem(tile + n_tile - 1 + 2 * side_far, n_tile), me), device_id_type=MESH
        )

    place = lax.rem(lane // 8 + 2 * sub, 16)
    spots = [place, lax.rem(place + 15, 16), place]
    frac = [zero, zero, zero]
    for source in range(TRC):
        rows = [jnp.broadcast_to(frecv[source, i : i + 1, :], (8, 128)) for i in (0, 0, 1)]
        frac = [jnp.where(spots[d] == source, rows[d], frac[d]) for d in range(3)]
    frac[1] = pltpu.roll(frac[1], 120, 1)
    weights = []
    for d in range(3):
        fd = pltpu.roll(frac[d], 0, 1, stride=16, stride_axis=0)
        weights.append(taps(fd, oin[8 * d : 8 * d + 8, :] == -1))
    cross, levels, along = weights
    upper = lax.rem(sub, 2) == 1
    level0 = levels[0] + levels[1] + jnp.where(upper, zero, levels[2])
    level1 = levels[3] + levels[4] + jnp.where(upper, levels[2], zero)
    for a in range(5):
        for level, lw in enumerate((level0, level1)):
            pair = cross[a] * lw
            for b in range(5):
                w = pair * along[b]
                if b != 2:
                    w = pltpu.roll(w, (b - 2) % 128, 1)
                wbuf[(b * 5 + a) * 2 + level] = w

    def first(k, carry):
        side = lax.rem(side_far + k // 2, 2)
        x = 2 * side + lax.rem(k, 2)
        moved = transport(src1, wbuf, x)
        for l in range(2):
            for g in range(4):
                src2[4 + 2 * x + l, pl.ds(8 * g, 8), :] = moved[l][g]
        moved_halo(side, lax.rem(k, 2)).start()
        return carry

    lax.fori_loop(0, 4, first, 0)

    def rim(side):
        for i in range(2):
            moved_halo(1 - side, i).wait_recv()
        turn(src2, side)

    zs = [lax.rem(z_me + 1 + quad // 2 + i, SIDE) for i in range(SIDE)]

    def pack(moved, x):
        for l in range(2):
            for g in range(2):
                even, odd = moved[l][g], moved[l][2 + g]
                at = pl.ds(8 * g, 8)
                send2[4 * x + 2 * l, at, :] = jnp.where(low, even, pltpu.roll(odd, 64, 1))
                send2[4 * x + 2 * l + 1, at, :] = jnp.where(low, pltpu.roll(even, 64, 1), odd)

    def leave(side):
        near = lax.rem(x_me + 5 - 2 * side, SIDE) // 2
        for k in range(2):
            x = 2 * side + lax.rem(1 - near + k, 2)
            for i in range(SIDE):
                spread(send2, recv2, s2_sem, r2_sem, 4 * x + zs[i]).start()

    def early(k, carry):
        x = 2 * (1 - side_far) + k
        pack(transport(src2, wbuf, x), x)
        return carry

    rim(1 - side_far)
    lax.fori_loop(0, 2, early, 0)

    steps = [4 * side_far + n * (1 - 2 * side_far) for n in range(5)]
    cells = ((3 * side_far, 2), (1 + side_far, 1))
    for i, (x, reach) in enumerate(cells):
        moved = transport(src2, wbuf, x, steps[reach:])
        for l in range(2):
            for g in range(4):
                part[2 * i + l, pl.ds(8 * g, 8), :] = moved[l][g]

    @pl.when(inner)
    def _():
        pl.semaphore_wait(known_sem, 1)

    for i in range(2):
        moved_halo(1 - side_far, i).wait_recv()
    leave(1 - side_far)
    turn(src2, side_far)
    for i, (x, reach) in enumerate(cells):
        moved = [[part[2 * i + l, pl.ds(8 * g, 8), :] for g in range(4)] for l in range(2)]
        pack(transport(src2, wbuf, x, steps[:reach], moved), x)
    leave(side_far)

    sources = [4 * plane(k) + lax.rem(z_me + quad // 2 + 3 + i, SIDE) for k in (3, 2, 1, 0) for i in range(SIDE)]
    for k in range(SIDE):
        group = sources[SIDE * k : SIDE * k + SIDE]
        for source in group:
            arrived(recv2, r2_sem, s2_sem, source).wait_recv()
        for source in group:
            nbuf[pl.ds(source, 1), :] = jnp.sum(jnp.abs(recv2[source]), axis=0, keepdims=True)
    number = nbuf[...]
    low16 = lax.broadcasted_iota(jnp.int32, (16, 128), 1) < 64
    other = pltpu.roll(number, 64, 1)
    none = jnp.zeros_like(number)
    nums = jnp.concatenate(
        [
            jnp.where(low16, number, none),
            jnp.where(low16, other, none),
            jnp.where(low16, none, other),
            jnp.where(low16, none, number),
        ],
        axis=0,
    )
    coarse = nums.astype(jnp.bfloat16)
    fine = (nums - coarse.astype(jnp.float32)).astype(jnp.bfloat16)
    nums = jnp.concatenate([coarse, fine, coarse, fine], axis=0)

    def rates(start, count):
        found = jnp.dot(
            abuf[start : start + count].reshape(count * 16, 256), nums, preferred_element_type=jnp.float32
        )
        tbuf[start : start + count] = found.reshape(count, 16, 128)

    def gain(z):
        acc = [[None] * 2 for _ in range(8)]
        for i in range(TRC):
            m = [recv2[i, 0:8, :], recv2[i, 8:16, :]]
            for b in range(8):
                t = jnp.broadcast_to(tbuf[1 + 8 * z + b, i : i + 1, :], (8, 128))
                for h in range(2):
                    term = t * m[h]
                    acc[b][h] = term if acc[b][h] is None else acc[b][h] + term
        for x in range(SIDE):
            g = 4 * x + z
            rec = jnp.broadcast_to(rbuf[g : g + 1, :], (8, 128))
            for h in range(2):
                even, odd = acc[2 * x][h], acc[2 * x + 1][h]
                gained = jnp.where(low, even, odd) + pltpu.roll(jnp.where(low, odd, even), 64, 1)
                send3[g, 8 * h : 8 * h + 8, :] = (recv2[g, 8 * h : 8 * h + 8, :] + gained) * rec
        for i in (2, 1, 3, 0):
            spread(send3, recv3, s3_sem, r3_sem, 4 * lax.rem(x_me + i, SIDE) + z).start()

    rates(0, 9)
    rbuf[...] = 1.0 / (1.0 + tbuf[0])
    for z in range(SIDE):
        if z < SIDE - 1:
            rates(9 + 8 * z, 8)
        gain(z)

    for dest in others:
        share(dest).wait_send()
    for side in range(2):
        halo(side).wait_send()
        for i in range(2):
            moved_halo(side, i).wait_send()
    for dest in range(TRC):
        spread(send2, recv2, s2_sem, r2_sem, dest).wait_send()
    for dest in range(TRC):
        spread(send3, recv3, s3_sem, r3_sem, dest).wait_send()
    for k in (3, 2, 1, 0):
        x = plane(k)
        for z in range(SIDE):
            arrived(recv3, r3_sem, s3_sem, 4 * x + z).wait_recv()
        for i in range(2):
            r = 2 * x + i
            for h in range(2):
                c0, c1 = recv3[2 * r, 8 * h : 8 * h + 8, :], recv3[2 * r + 1, 8 * h : 8 * h + 8, :]
                out[pl.ds(64 * h + r, 8, stride=8), :] = jnp.where(low, c0, pltpu.roll(c1, 64, 1))
                out[pl.ds(128 + 64 * h + r, 8, stride=8), :] = jnp.where(low, pltpu.roll(c0, 64, 1), c1)


def solution(mesh):
    n_tile = mesh.shape["tile"]
    f32, i32, bf16 = jnp.float32, jnp.int32, jnp.bfloat16
    anywhere = pl.BlockSpec(memory_space=pltpu.HBM)

    def on_device(tracers, courant, shear, offsets, seam_flips, kernel, coag_target):
        result = pl.pallas_call(
            functools.partial(body, n_tile),
            out_shape=jax.ShapeDtypeStruct((256, 128), f32),
            in_specs=[anywhere] * 7,
            out_specs=pl.BlockSpec(memory_space=pltpu.VMEM),
            scratch_shapes=[
                pltpu.VMEM((256, 128), f32),
                pltpu.VMEM((24, 8), f32),
                pltpu.VMEM((24, 8), f32),
                pltpu.VMEM((24, 128), i32),
                pltpu.SMEM((32,), i32),
                pltpu.VMEM((32, 32), f32),
                pltpu.VMEM((32, 32), i32),
                pltpu.VMEM((24, 128), f32),
                pltpu.VMEM((2, 128), f32),
                pltpu.VMEM((TRC, 2, 128), f32),
                pltpu.VMEM((50, 8, 128), f32),
                pltpu.VMEM((16, 32, 128), f32),
                pltpu.VMEM((16, 32, 128), f32),
                pltpu.VMEM((4, 32, 128), f32),
                pltpu.VMEM((TRC, 16, 128), f32),
                pltpu.VMEM((TRC, 16, 128), f32),
                pltpu.VMEM((BINS + 1, 16, 256), bf16),
                pltpu.VMEM((16, 128), f32),
                pltpu.VMEM((BINS + 1, 16, 128), f32),
                pltpu.VMEM((16, 128), f32),
                pltpu.VMEM((TRC, 16, 128), f32),
                pltpu.VMEM((TRC, 16, 128), f32),
                pltpu.SemaphoreType.DMA((7,)),
                pltpu.SemaphoreType.DMA((3, 2)),
                pltpu.SemaphoreType.DMA((3, 2)),
                pltpu.SemaphoreType.DMA((TRC,)),
                pltpu.SemaphoreType.DMA((TRC,)),
                pltpu.SemaphoreType.REGULAR,
                pltpu.SemaphoreType.DMA((TRC,)),
                pltpu.SemaphoreType.DMA((TRC,)),
                pltpu.SemaphoreType.DMA((TRC,)),
                pltpu.SemaphoreType.DMA((TRC,)),
            ],
            compiler_params=pltpu.CompilerParams(
                collective_id=0, has_side_effects=True, vmem_limit_bytes=48 * 1024 * 1024
            ),
        )(
            *(
                pltpu.with_memory_space_constraint(v, pltpu.HBM)
                for v in (
                    tracers.reshape(256, 128), courant.reshape(24, 8), shear.reshape(24, 8),
                    offsets.reshape(24, 128), seam_flips, kernel, coag_target,
                )
            ),
        )
        return result.reshape(32, 4, 2, 128)

    return jax.shard_map(
        on_device,
        mesh=mesh,
        in_specs=(
            P("trc", "tile", None, None),
            P(None, "tile", None, "trc"),
            P(None, "tile", None, "trc"),
            P(None, "tile", None, None),
            P(),
            P(),
            P(),
        ),
        out_specs=P("trc", "tile", None, None),
        check_vma=False,
    )
```

```python
import functools

import jax
import jax.numpy as jnp
from jax import lax
from jax.experimental import pallas as pl
from jax.experimental.pallas import tpu as pltpu
from jax.sharding import PartitionSpec as P

BINS = 32
COMPS = 16
ITER = 3
TRC = 16
SIDE = 4
MESH = pl.DeviceIdType.MESH
EXACT = lax.Precision.HIGHEST


def taps(f, lower):
    p0 = -f * (f - 1.0) * (f - 2.0) / 6.0
    p1 = (f + 1.0) * (f - 1.0) * (f - 2.0) / 2.0
    p2 = -(f + 1.0) * f * (f - 2.0) / 2.0
    p3 = (f + 1.0) * f * (f - 1.0) / 6.0
    zero = jnp.zeros_like(f)
    return [
        jnp.where(lower, p0, zero),
        jnp.where(lower, p1, p0),
        jnp.where(lower, p2, p1),
        jnp.where(lower, p3, p2),
        jnp.where(lower, zero, p3),
    ]


def transport(src, wbuf, x, steps=range(5), out=None):
    for b in range(5):
        acc = [[None] * 4, [None] * 4]
        for a in steps:
            for level in range(2):
                q = [src[2 * x + 2 * a + level, pl.ds(8 * g, 8), :] for g in range(4)]
                for l in range(2):
                    w = wbuf[(b * 5 + a) * 2 + level, pl.ds(2 * x + l, 1), :]
                    w = jnp.broadcast_to(w, (8, 128))
                    for g in range(4):
                        term = w * q[g]
                        acc[l][g] = term if acc[l][g] is None else acc[l][g] + term
        if b != 2:
            acc = [[pltpu.roll(v, (2 - b) % 128, 1) for v in row] for row in acc]
        out = acc if out is None else [[o + v for o, v in zip(r, s)] for r, s in zip(out, acc)]
    return out


def body(
    n_tile, tr, co, sh, of, fi, ke, ct, out,
    tin, cin, sin, oin, fl, kin, ctin, fpad, fsend, frecv, wbuf, src1, src2, part,
    send2, recv2, abuf, nbuf, tbuf, rbuf, send3, recv3,
    in_sem, hs_sem, hr_sem, fs_sem, fr_sem, known_sem, s2_sem, r2_sem, s3_sem, r3_sem,
):
    tile, me = lax.axis_index("tile"), lax.axis_index("trc")
    x_me, z_me = me // SIDE, lax.rem(me, SIDE)
    prev = lax.rem(tile + n_tile - 1, n_tile)
    after = lax.rem(tile + 1, n_tile)

    quad = lax.rem(tile, 4)
    side_far = lax.rem(quad, 2)
    partner = tile + 2 - 4 * (quad // 2)

    def plane(k):
        return lax.rem(x_me + 6 - k + 3 * (k // 2) + 2 * (k // 3), SIDE)

    others = [4 * plane(k) + lax.rem(z_me + i, SIDE) for k in range(SIDE) for i in (2, 1, 3, 0)][:-1]
    barrier = pltpu.get_barrier_semaphore()
    for dest in others:
        pl.semaphore_signal(barrier, inc=1, device_id=(tile, dest), device_id_type=MESH)
    for t in (prev, after):
        pl.semaphore_signal(barrier, inc=1, device_id=(t, me), device_id_type=MESH)

    loads = [
        pltpu.make_async_copy(s, d, in_sem.at[i])
        for i, (s, d) in enumerate(
            ((co, cin), (sh, sin), (tr, tin), (of, oin), (ke, kin), (ct, ctin), (fi, fl))
        )
    ]
    for load in loads:
        load.start()

    lane = lax.broadcasted_iota(jnp.int32, (8, 128), 1)
    sub = lax.broadcasted_iota(jnp.int32, (8, 128), 0)
    low = lane < 64

    fpad[...] = jnp.zeros_like(fpad)
    loads[0].wait()
    loads[1].wait()
    c, s = cin[...], sin[...]
    f = jnp.full(c.shape, 0.5, jnp.float32)
    for _ in range(ITER):
        f = jax.nn.sigmoid(c + s * (f - 0.5))
    fpad[:, 0:8] = f
    zero = jnp.zeros((8, 128), jnp.float32)
    rows = []
    for packed in (fpad[0:8] + pltpu.roll(fpad[8:16], 8, 1), fpad[16:24]):
        for bit in (1, 2, 4):
            packed = jnp.where(lax.rem(sub // bit, 2) == 1, pltpu.roll(packed, 128 - 16 * bit, 1), packed)
        packed = pltpu.roll(packed, me * 8, 1)
        rows.append(jnp.sum(packed, axis=0, keepdims=True))
    top, bottom = rows
    fsend[0:1, :] = top
    fsend[1:2, :] = bottom
    frecv[me, 0:1, :] = top
    frecv[me, 1:2, :] = bottom

    loads[2].wait()
    for r in range(8):
        for g in range(4):
            src1[4 + r, pl.ds(8 * g, 8), :] = tin[pl.ds(64 * g + r, 8, stride=8), :]

    pl.semaphore_wait(barrier, TRC + 1)

    def halo(side):
        return pltpu.make_async_remote_copy(
            src_ref=src1.at[pl.ds(4 + 4 * side, 4)],
            dst_ref=src1.at[pl.ds(12 - 12 * side, 4)],
            send_sem=hs_sem.at[0, side],
            recv_sem=hr_sem.at[0, side],
            device_id=((prev, after)[side], me),
            device_id_type=MESH,
        )

    def moved_halo(side, i):
        return pltpu.make_async_remote_copy(
            src_ref=src2.at[pl.ds(4 + 4 * side + 2 * i, 2)],
            dst_ref=src2.at[pl.ds(12 - 12 * side + 2 * i, 2)],
            send_sem=hs_sem.at[1 + i, side],
            recv_sem=hr_sem.at[1 + i, side],
            device_id=(lax.rem(tile + n_tile - 1 + 2 * side, n_tile), me),
            device_id_type=MESH,
        )

    def share(dest):
        return pltpu.make_async_remote_copy(
            src_ref=fsend, dst_ref=frecv.at[me], send_sem=fs_sem.at[dest], recv_sem=fr_sem.at[me],
            device_id=(tile, dest), device_id_type=MESH,
        )

    def spread(src, dst, s_sem, r_sem, dest):
        return pltpu.make_async_remote_copy(
            src_ref=src.at[dest], dst_ref=dst.at[me], send_sem=s_sem.at[dest], recv_sem=r_sem.at[me],
            device_id=(partner, dest), device_id_type=MESH,
        )

    def arrived(dst, r_sem, s_sem, source):
        return pltpu.make_async_remote_copy(
            src_ref=dst.at[source], dst_ref=dst.at[source], send_sem=s_sem.at[source],
            recv_sem=r_sem.at[source], device_id=(tile, source), device_id_type=MESH,
        )

    for z in (3, 2, 1, 0):
        for i in (2, 1, 3, 0):
            dest = 4 * lax.rem(x_me + i, SIDE) + z

            @pl.when(dest != me)
            def _(dest=dest):
                share(dest).start()

    halo(0).start()
    halo(1).start()

    loads[4].wait()
    loads[5].wait()
    spot = lax.broadcasted_iota(jnp.int32, (32, 256), 1)
    j = lax.broadcasted_iota(jnp.int32, (32, 256), 0)
    at = lax.rem(j, 2) * 16 + j // 2
    rate = jnp.zeros((16, 256), jnp.float32)
    target = jnp.zeros((16, 256), jnp.float32)
    for p in range(2):
        place = (lax.rem(spot, 64) == at + 32 * p).astype(jnp.float32)
        rate += jnp.dot(kin[pl.ds(p, 16, stride=2), :], place, precision=EXACT, preferred_element_type=jnp.float32)
        target += jnp.dot(
            ctin[pl.ds(p, 16, stride=2), :].astype(jnp.float32), place, precision=EXACT,
            preferred_element_type=jnp.float32,
        )
    coarse = rate.astype(jnp.bfloat16).astype(jnp.float32)
    rate = jnp.where(lax.broadcasted_iota(jnp.int32, (16, 256), 1) < 128, coarse, rate - coarse)

    def fill(b, carry):
        hit = jnp.abs(target - b.astype(jnp.float32)) < 0.5
        abuf[1 + 8 * (lax.rem(b, 8) // 2) + 2 * (b // 8) + lax.rem(b, 2)] = jnp.where(hit, rate, 0.0).astype(jnp.bfloat16)
        return carry

    lax.fori_loop(0, BINS, fill, 0)
    abuf[0] = rate.astype(jnp.bfloat16)

    mirror = 127 - lane
    loads[6].wait()

    def turn(buf, side):
        turned = jnp.full((8, 128), fl[lax.rem(tile + side, n_tile)], jnp.int32) == 1
        for i in range(4):
            for g in range(4):
                at = (12 * side + i, pl.ds(8 * g, 8), slice(None))
                v = buf[at]
                buf[at] = jnp.where(turned, jnp.take_along_axis(v, mirror, axis=1), v)

    for side in range(2):
        halo(1 - side).wait_recv()
        turn(src1, side)

    loads[3].wait()
    for source in others:
        arrived(frecv, fr_sem, fs_sem, source).wait_recv()

    inner = (quad + 1) // 2 == 1

    @pl.when(inner)
    def _():
        pl.semaphore_signal(
            known_sem, inc=1, device_id=(lax.rem(tile + n_tile - 1 + 2 * side_far, n_tile), me), device_id_type=MESH
        )

    place = lax.rem(lane // 8 + 2 * sub, 16)
    spots = [place, lax.rem(place + 15, 16), place]
    frac = [zero, zero, zero]
    for source in range(TRC):
        rows = [jnp.broadcast_to(frecv[source, i : i + 1, :], (8, 128)) for i in (0, 0, 1)]
        frac = [jnp.where(spots[d] == source, rows[d], frac[d]) for d in range(3)]
    frac[1] = pltpu.roll(frac[1], 120, 1)
    weights = []
    for d in range(3):
        fd = pltpu.roll(frac[d], 0, 1, stride=16, stride_axis=0)
        weights.append(taps(fd, oin[8 * d : 8 * d + 8, :] == -1))
    cross, levels, along = weights
    upper = lax.rem(sub, 2) == 1
    level0 = levels[0] + levels[1] + jnp.where(upper, zero, levels[2])
    level1 = levels[3] + levels[4] + jnp.where(upper, levels[2], zero)
    for a in range(5):
        for level, lw in enumerate((level0, level1)):
            pair = cross[a] * lw
            for b in range(5):
                w = pair * along[b]
                if b != 2:
                    w = pltpu.roll(w, (b - 2) % 128, 1)
                wbuf[(b * 5 + a) * 2 + level] = w

    def first(k, carry):
        side = lax.rem(side_far + k // 2, 2)
        x = 2 * side + lax.rem(k, 2)
        moved = transport(src1, wbuf, x)
        for l in range(2):
            for g in range(4):
                src2[4 + 2 * x + l, pl.ds(8 * g, 8), :] = moved[l][g]
        moved_halo(side, lax.rem(k, 2)).start()
        return carry

    lax.fori_loop(0, 4, first, 0)

    def rim(side):
        for i in range(2):
            moved_halo(1 - side, i).wait_recv()
        turn(src2, side)

    zs = [lax.rem(z_me + 1 + quad // 2 + i, SIDE) for i in range(SIDE)]

    def pack(moved, x):
        for l in range(2):
            for g in range(2):
                even, odd = moved[l][g], moved[l][2 + g]
                at = pl.ds(8 * g, 8)
                send2[4 * x + 2 * l, at, :] = jnp.where(low, even, pltpu.roll(odd, 64, 1))
                send2[4 * x + 2 * l + 1, at, :] = jnp.where(low, pltpu.roll(even, 64, 1), odd)

    def leave(side):
        near = lax.rem(x_me + 5 - 2 * side, SIDE) // 2
        for k in range(2):
            x = 2 * side + lax.rem(1 - near + k, 2)
            for i in range(SIDE):
                spread(send2, recv2, s2_sem, r2_sem, 4 * x + zs[i]).start()

    def early(k, carry):
        x = 2 * (1 - side_far) + k
        pack(transport(src2, wbuf, x), x)
        return carry

    rim(1 - side_far)
    lax.fori_loop(0, 2, early, 0)

    steps = [4 * side_far + n * (1 - 2 * side_far) for n in range(5)]
    cells = ((3 * side_far, 2), (1 + side_far, 1))
    for i, (x, reach) in enumerate(cells):
        moved = transport(src2, wbuf, x, steps[reach:])
        for l in range(2):
            for g in range(4):
                part[2 * i + l, pl.ds(8 * g, 8), :] = moved[l][g]

    @pl.when(inner)
    def _():
        pl.semaphore_wait(known_sem, 1)

    for i in range(2):
        moved_halo(1 - side_far, i).wait_recv()
    turn(src2, side_far)
    for i, (x, reach) in enumerate(cells):
        moved = [[part[2 * i + l, pl.ds(8 * g, 8), :] for g in range(4)] for l in range(2)]
        pack(transport(src2, wbuf, x, steps[:reach], moved), x)
    for half in range(2):
        for k in range(SIDE):
            for i in range(2):
                spread(send2, recv2, s2_sem, r2_sem, 4 * plane(k) + zs[2 * half + i]).start()

    sources = [4 * plane(k) + lax.rem(z_me + quad // 2 + 3 + i, SIDE) for k in (3, 2, 1, 0) for i in range(SIDE)]
    for k in range(SIDE):
        group = sources[SIDE * k : SIDE * k + SIDE]
        for source in group:
            arrived(recv2, r2_sem, s2_sem, source).wait_recv()
        for source in group:
            nbuf[pl.ds(source, 1), :] = jnp.sum(jnp.abs(recv2[source]), axis=0, keepdims=True)
    number = nbuf[...]
    low16 = lax.broadcasted_iota(jnp.int32, (16, 128), 1) < 64
    other = pltpu.roll(number, 64, 1)
    none = jnp.zeros_like(number)
    nums = jnp.concatenate(
        [
            jnp.where(low16, number, none),
            jnp.where(low16, other, none),
            jnp.where(low16, none, other),
            jnp.where(low16, none, number),
        ],
        axis=0,
    )
    coarse = nums.astype(jnp.bfloat16)
    fine = (nums - coarse.astype(jnp.float32)).astype(jnp.bfloat16)
    nums = jnp.concatenate([coarse, fine, coarse, fine], axis=0)

    def rates(start, count):
        found = jnp.dot(
            abuf[start : start + count].reshape(count * 16, 256), nums, preferred_element_type=jnp.float32
        )
        tbuf[start : start + count] = found.reshape(count, 16, 128)

    def gain(z):
        acc = [[None] * 2 for _ in range(8)]
        for i in range(TRC):
            m = [recv2[i, 0:8, :], recv2[i, 8:16, :]]
            for b in range(8):
                t = jnp.broadcast_to(tbuf[1 + 8 * z + b, i : i + 1, :], (8, 128))
                for h in range(2):
                    term = t * m[h]
                    acc[b][h] = term if acc[b][h] is None else acc[b][h] + term
        for x in range(SIDE):
            g = 4 * x + z
            rec = jnp.broadcast_to(rbuf[g : g + 1, :], (8, 128))
            for h in range(2):
                even, odd = acc[2 * x][h], acc[2 * x + 1][h]
                gained = jnp.where(low, even, odd) + pltpu.roll(jnp.where(low, odd, even), 64, 1)
                send3[g, 8 * h : 8 * h + 8, :] = (recv2[g, 8 * h : 8 * h + 8, :] + gained) * rec
        for i in (2, 1, 3, 0):
            spread(send3, recv3, s3_sem, r3_sem, 4 * lax.rem(x_me + i, SIDE) + z).start()

    rates(0, 9)
    rbuf[...] = 1.0 / (1.0 + tbuf[0])
    for z in range(SIDE):
        if z < SIDE - 1:
            rates(9 + 8 * z, 8)
        gain(z)

    for dest in others:
        share(dest).wait_send()
    for side in range(2):
        halo(side).wait_send()
        for i in range(2):
            moved_halo(side, i).wait_send()
    for dest in range(TRC):
        spread(send2, recv2, s2_sem, r2_sem, dest).wait_send()
    for dest in range(TRC):
        spread(send3, recv3, s3_sem, r3_sem, dest).wait_send()
    for k in (3, 2, 1, 0):
        x = plane(k)
        for z in range(SIDE):
            arrived(recv3, r3_sem, s3_sem, 4 * x + z).wait_recv()
        for i in range(2):
            r = 2 * x + i
            for h in range(2):
                c0, c1 = recv3[2 * r, 8 * h : 8 * h + 8, :], recv3[2 * r + 1, 8 * h : 8 * h + 8, :]
                out[pl.ds(64 * h + r, 8, stride=8), :] = jnp.where(low, c0, pltpu.roll(c1, 64, 1))
                out[pl.ds(128 + 64 * h + r, 8, stride=8), :] = jnp.where(low, pltpu.roll(c0, 64, 1), c1)


def solution(mesh):
    n_tile = mesh.shape["tile"]
    f32, i32, bf16 = jnp.float32, jnp.int32, jnp.bfloat16
    anywhere = pl.BlockSpec(memory_space=pltpu.HBM)

    def on_device(tracers, courant, shear, offsets, seam_flips, kernel, coag_target):
        result = pl.pallas_call(
            functools.partial(body, n_tile),
            out_shape=jax.ShapeDtypeStruct((256, 128), f32),
            in_specs=[anywhere] * 7,
            out_specs=pl.BlockSpec(memory_space=pltpu.VMEM),
            scratch_shapes=[
                pltpu.VMEM((256, 128), f32),
                pltpu.VMEM((24, 8), f32),
                pltpu.VMEM((24, 8), f32),
                pltpu.VMEM((24, 128), i32),
                pltpu.SMEM((32,), i32),
                pltpu.VMEM((32, 32), f32),
                pltpu.VMEM((32, 32), i32),
                pltpu.VMEM((24, 128), f32),
                pltpu.VMEM((2, 128), f32),
                pltpu.VMEM((TRC, 2, 128), f32),
                pltpu.VMEM((50, 8, 128), f32),
                pltpu.VMEM((16, 32, 128), f32),
                pltpu.VMEM((16, 32, 128), f32),
                pltpu.VMEM((4, 32, 128), f32),
                pltpu.VMEM((TRC, 16, 128), f32),
                pltpu.VMEM((TRC, 16, 128), f32),
                pltpu.VMEM((BINS + 1, 16, 256), bf16),
                pltpu.VMEM((16, 128), f32),
                pltpu.VMEM((BINS + 1, 16, 128), f32),
                pltpu.VMEM((16, 128), f32),
                pltpu.VMEM((TRC, 16, 128), f32),
                pltpu.VMEM((TRC, 16, 128), f32),
                pltpu.SemaphoreType.DMA((7,)),
                pltpu.SemaphoreType.DMA((3, 2)),
                pltpu.SemaphoreType.DMA((3, 2)),
                pltpu.SemaphoreType.DMA((TRC,)),
                pltpu.SemaphoreType.DMA((TRC,)),
                pltpu.SemaphoreType.REGULAR,
                pltpu.SemaphoreType.DMA((TRC,)),
                pltpu.SemaphoreType.DMA((TRC,)),
                pltpu.SemaphoreType.DMA((TRC,)),
                pltpu.SemaphoreType.DMA((TRC,)),
            ],
            compiler_params=pltpu.CompilerParams(
                collective_id=0, has_side_effects=True, vmem_limit_bytes=48 * 1024 * 1024
            ),
        )(
            *(
                pltpu.with_memory_space_constraint(v, pltpu.HBM)
                for v in (
                    tracers.reshape(256, 128), courant.reshape(24, 8), shear.reshape(24, 8),
                    offsets.reshape(24, 128), seam_flips, kernel, coag_target,
                )
            ),
        )
        return result.reshape(32, 4, 2, 128)

    return jax.shard_map(
        on_device,
        mesh=mesh,
        in_specs=(
            P("trc", "tile", None, None),
            P(None, "tile", None, "trc"),
            P(None, "tile", None, "trc"),
            P(None, "tile", None, None),
            P(),
            P(),
            P(),
        ),
        out_specs=P("trc", "tile", None, None),
        check_vma=False,
    )
```

```python
import functools

import jax
import jax.numpy as jnp
from jax import lax
from jax.experimental import pallas as pl
from jax.experimental.pallas import tpu as pltpu
from jax.sharding import PartitionSpec as P

BINS = 32
COMPS = 16
ITER = 3
TRC = 16
SIDE = 4
MESH = pl.DeviceIdType.MESH
EXACT = lax.Precision.HIGHEST


def taps(f, lower):
    p0 = -f * (f - 1.0) * (f - 2.0) / 6.0
    p1 = (f + 1.0) * (f - 1.0) * (f - 2.0) / 2.0
    p2 = -(f + 1.0) * f * (f - 2.0) / 2.0
    p3 = (f + 1.0) * f * (f - 1.0) / 6.0
    zero = jnp.zeros_like(f)
    return [
        jnp.where(lower, p0, zero),
        jnp.where(lower, p1, p0),
        jnp.where(lower, p2, p1),
        jnp.where(lower, p3, p2),
        jnp.where(lower, zero, p3),
    ]


def transport(src, wbuf, x, steps=range(5), out=None):
    for b in range(5):
        acc = [[None] * 4, [None] * 4]
        for a in steps:
            for level in range(2):
                q = [src[2 * x + 2 * a + level, pl.ds(8 * g, 8), :] for g in range(4)]
                for l in range(2):
                    w = wbuf[(b * 5 + a) * 2 + level, pl.ds(2 * x + l, 1), :]
                    w = jnp.broadcast_to(w, (8, 128))
                    for g in range(4):
                        term = w * q[g]
                        acc[l][g] = term if acc[l][g] is None else acc[l][g] + term
        if b != 2:
            acc = [[pltpu.roll(v, (2 - b) % 128, 1) for v in row] for row in acc]
        out = acc if out is None else [[o + v for o, v in zip(r, s)] for r, s in zip(out, acc)]
    return out


def body(
    n_tile, tr, co, sh, of, fi, ke, ct, out,
    tin, cin, sin, oin, fl, kin, ctin, fpad, fsend, frecv, wbuf, src1, src2, part,
    send2, recv2, abuf, nbuf, tbuf, rbuf, send3, recv3,
    in_sem, hs_sem, hr_sem, fs_sem, fr_sem, known_sem, s2_sem, r2_sem, s3_sem, r3_sem,
):
    tile, me = lax.axis_index("tile"), lax.axis_index("trc")
    x_me, z_me = me // SIDE, lax.rem(me, SIDE)
    prev = lax.rem(tile + n_tile - 1, n_tile)
    after = lax.rem(tile + 1, n_tile)

    quad = lax.rem(tile, 4)
    side_far = lax.rem(quad, 2)
    partner = tile + 2 - 4 * (quad // 2)

    def plane(k):
        return lax.rem(x_me + 6 - k + 3 * (k // 2) + 2 * (k // 3), SIDE)

    others = [4 * plane(k) + lax.rem(z_me + i, SIDE) for k in range(SIDE) for i in (2, 1, 3, 0)][:-1]
    barrier = pltpu.get_barrier_semaphore()
    for dest in others:
        pl.semaphore_signal(barrier, inc=1, device_id=(tile, dest), device_id_type=MESH)
    for t in (prev, after):
        pl.semaphore_signal(barrier, inc=1, device_id=(t, me), device_id_type=MESH)

    loads = [
        pltpu.make_async_copy(s, d, in_sem.at[i])
        for i, (s, d) in enumerate(
            ((co, cin), (sh, sin), (tr, tin), (of, oin), (ke, kin), (ct, ctin), (fi, fl))
        )
    ]
    for load in loads:
        load.start()

    lane = lax.broadcasted_iota(jnp.int32, (8, 128), 1)
    sub = lax.broadcasted_iota(jnp.int32, (8, 128), 0)
    low = lane < 64

    fpad[...] = jnp.zeros_like(fpad)
    loads[0].wait()
    loads[1].wait()
    c, s = cin[...], sin[...]
    f = jnp.full(c.shape, 0.5, jnp.float32)
    for _ in range(ITER):
        f = jax.nn.sigmoid(c + s * (f - 0.5))
    fpad[:, 0:8] = f
    zero = jnp.zeros((8, 128), jnp.float32)
    rows = []
    for packed in (fpad[0:8] + pltpu.roll(fpad[8:16], 8, 1), fpad[16:24]):
        for bit in (1, 2, 4):
            packed = jnp.where(lax.rem(sub // bit, 2) == 1, pltpu.roll(packed, 128 - 16 * bit, 1), packed)
        packed = pltpu.roll(packed, me * 8, 1)
        rows.append(jnp.sum(packed, axis=0, keepdims=True))
    top, bottom = rows
    fsend[0:1, :] = top
    fsend[1:2, :] = bottom
    frecv[me, 0:1, :] = top
    frecv[me, 1:2, :] = bottom

    loads[2].wait()
    for r in range(8):
        for g in range(4):
            src1[4 + r, pl.ds(8 * g, 8), :] = tin[pl.ds(64 * g + r, 8, stride=8), :]

    pl.semaphore_wait(barrier, TRC + 1)

    def halo(side):
        return pltpu.make_async_remote_copy(
            src_ref=src1.at[pl.ds(4 + 4 * side, 4)],
            dst_ref=src1.at[pl.ds(12 - 12 * side, 4)],
            send_sem=hs_sem.at[0, side],
            recv_sem=hr_sem.at[0, side],
            device_id=((prev, after)[side], me),
            device_id_type=MESH,
        )

    def moved_halo(side, i):
        return pltpu.make_async_remote_copy(
            src_ref=src2.at[pl.ds(4 + 4 * side + 2 * i, 2)],
            dst_ref=src2.at[pl.ds(12 - 12 * side + 2 * i, 2)],
            send_sem=hs_sem.at[1 + i, side],
            recv_sem=hr_sem.at[1 + i, side],
            device_id=(lax.rem(tile + n_tile - 1 + 2 * side, n_tile), me),
            device_id_type=MESH,
        )

    def share(dest):
        return pltpu.make_async_remote_copy(
            src_ref=fsend, dst_ref=frecv.at[me], send_sem=fs_sem.at[dest], recv_sem=fr_sem.at[me],
            device_id=(tile, dest), device_id_type=MESH,
        )

    def spread(src, dst, s_sem, r_sem, dest):
        return pltpu.make_async_remote_copy(
            src_ref=src.at[dest], dst_ref=dst.at[me], send_sem=s_sem.at[dest], recv_sem=r_sem.at[me],
            device_id=(partner, dest), device_id_type=MESH,
        )

    def arrived(dst, r_sem, s_sem, source):
        return pltpu.make_async_remote_copy(
            src_ref=dst.at[source], dst_ref=dst.at[source], send_sem=s_sem.at[source],
            recv_sem=r_sem.at[source], device_id=(tile, source), device_id_type=MESH,
        )

    for z in (3, 2, 1, 0):
        for i in (2, 1, 3, 0):
            dest = 4 * lax.rem(x_me + i, SIDE) + z

            @pl.when(dest != me)
            def _(dest=dest):
                share(dest).start()

    halo(0).start()
    halo(1).start()

    loads[4].wait()
    loads[5].wait()
    spot = lax.broadcasted_iota(jnp.int32, (32, 256), 1)
    j = lax.broadcasted_iota(jnp.int32, (32, 256), 0)
    at = lax.rem(j, 2) * 16 + j // 2
    rate = jnp.zeros((16, 256), jnp.float32)
    target = jnp.zeros((16, 256), jnp.float32)
    for p in range(2):
        place = (lax.rem(spot, 64) == at + 32 * p).astype(jnp.float32)
        rate += jnp.dot(kin[pl.ds(p, 16, stride=2), :], place, precision=EXACT, preferred_element_type=jnp.float32)
        target += jnp.dot(
            ctin[pl.ds(p, 16, stride=2), :].astype(jnp.float32), place, precision=EXACT,
            preferred_element_type=jnp.float32,
        )
    coarse = rate.astype(jnp.bfloat16).astype(jnp.float32)
    rate = jnp.where(lax.broadcasted_iota(jnp.int32, (16, 256), 1) < 128, coarse, rate - coarse)

    def fill(b, carry):
        hit = jnp.abs(target - b.astype(jnp.float32)) < 0.5
        abuf[1 + 8 * (lax.rem(b, 8) // 2) + 2 * (b // 8) + lax.rem(b, 2)] = jnp.where(hit, rate, 0.0).astype(jnp.bfloat16)
        return carry

    lax.fori_loop(0, BINS, fill, 0)
    abuf[0] = rate.astype(jnp.bfloat16)

    mirror = 127 - lane
    loads[6].wait()

    def turn(buf, side):
        turned = jnp.full((8, 128), fl[lax.rem(tile + side, n_tile)], jnp.int32) == 1
        for i in range(4):
            for g in range(4):
                at = (12 * side + i, pl.ds(8 * g, 8), slice(None))
                v = buf[at]
                buf[at] = jnp.where(turned, jnp.take_along_axis(v, mirror, axis=1), v)

    for side in range(2):
        halo(1 - side).wait_recv()
        turn(src1, side)

    loads[3].wait()
    place = lax.rem(lane // 8 + 2 * sub, 16)
    spots = [place, lax.rem(place + 15, 16), place]
    frac = [zero, zero, zero]
    for source in [me] + others[::-1]:
        if source is not me:
            arrived(frecv, fr_sem, fs_sem, source).wait_recv()
        rows = [jnp.broadcast_to(frecv[source, i : i + 1, :], (8, 128)) for i in (0, 0, 1)]
        frac = [jnp.where(spots[d] == source, rows[d], frac[d]) for d in range(3)]

    inner = (quad + 1) // 2 == 1

    @pl.when(inner)
    def _():
        pl.semaphore_signal(
            known_sem, inc=1, device_id=(lax.rem(tile + n_tile - 1 + 2 * side_far, n_tile), me), device_id_type=MESH
        )

    frac[1] = pltpu.roll(frac[1], 120, 1)
    weights = []
    for d in range(3):
        fd = pltpu.roll(frac[d], 0, 1, stride=16, stride_axis=0)
        weights.append(taps(fd, oin[8 * d : 8 * d + 8, :] == -1))
    cross, levels, along = weights
    upper = lax.rem(sub, 2) == 1
    level0 = levels[0] + levels[1] + jnp.where(upper, zero, levels[2])
    level1 = levels[3] + levels[4] + jnp.where(upper, levels[2], zero)
    for a in range(5):
        for level, lw in enumerate((level0, level1)):
            pair = cross[a] * lw
            for b in range(5):
                w = pair * along[b]
                if b != 2:
                    w = pltpu.roll(w, (b - 2) % 128, 1)
                wbuf[(b * 5 + a) * 2 + level] = w

    def first(k, carry):
        side = lax.rem(side_far + k // 2, 2)
        x = 2 * side + lax.rem(k, 2)
        moved = transport(src1, wbuf, x)
        for l in range(2):
            for g in range(4):
                src2[4 + 2 * x + l, pl.ds(8 * g, 8), :] = moved[l][g]
        moved_halo(side, lax.rem(k, 2)).start()
        return carry

    lax.fori_loop(0, 4, first, 0)

    def rim(side):
        for i in range(2):
            moved_halo(1 - side, i).wait_recv()
        turn(src2, side)

    zs = [lax.rem(z_me + 1 + quad // 2 + i, SIDE) for i in range(SIDE)]

    def pack(moved, x):
        for l in range(2):
            for g in range(2):
                even, odd = moved[l][g], moved[l][2 + g]
                at = pl.ds(8 * g, 8)
                send2[4 * x + 2 * l, at, :] = jnp.where(low, even, pltpu.roll(odd, 64, 1))
                send2[4 * x + 2 * l + 1, at, :] = jnp.where(low, pltpu.roll(even, 64, 1), odd)

    def leave(side):
        near = lax.rem(x_me + 5 - 2 * side, SIDE) // 2
        for k in range(2):
            x = 2 * side + lax.rem(1 - near + k, 2)
            for i in range(SIDE):
                spread(send2, recv2, s2_sem, r2_sem, 4 * x + zs[i]).start()

    def early(k, carry):
        x = 2 * (1 - side_far) + k
        pack(transport(src2, wbuf, x), x)
        return carry

    rim(1 - side_far)
    lax.fori_loop(0, 2, early, 0)

    steps = [4 * side_far + n * (1 - 2 * side_far) for n in range(5)]
    cells = ((3 * side_far, 2), (1 + side_far, 1))
    for i, (x, reach) in enumerate(cells):
        moved = transport(src2, wbuf, x, steps[reach:])
        for l in range(2):
            for g in range(4):
                part[2 * i + l, pl.ds(8 * g, 8), :] = moved[l][g]

    @pl.when(inner)
    def _():
        pl.semaphore_wait(known_sem, 1)

    for i in range(2):
        moved_halo(1 - side_far, i).wait_recv()
    turn(src2, side_far)
    for i, (x, reach) in enumerate(cells):
        moved = [[part[2 * i + l, pl.ds(8 * g, 8), :] for g in range(4)] for l in range(2)]
        pack(transport(src2, wbuf, x, steps[:reach], moved), x)
    for half in range(2):
        for k in range(SIDE):
            for i in range(2):
                spread(send2, recv2, s2_sem, r2_sem, 4 * plane(k) + zs[2 * half + i]).start()

    sources = [4 * plane(k) + lax.rem(z_me + quad // 2 + 3 + i, SIDE) for k in (3, 2, 1, 0) for i in range(SIDE)]
    for k in range(SIDE):
        group = sources[SIDE * k : SIDE * k + SIDE]
        for source in group:
            arrived(recv2, r2_sem, s2_sem, source).wait_recv()
        for source in group:
            nbuf[pl.ds(source, 1), :] = jnp.sum(jnp.abs(recv2[source]), axis=0, keepdims=True)
    number = nbuf[...]
    low16 = lax.broadcasted_iota(jnp.int32, (16, 128), 1) < 64
    other = pltpu.roll(number, 64, 1)
    none = jnp.zeros_like(number)
    nums = jnp.concatenate(
        [
            jnp.where(low16, number, none),
            jnp.where(low16, other, none),
            jnp.where(low16, none, other),
            jnp.where(low16, none, number),
        ],
        axis=0,
    )
    coarse = nums.astype(jnp.bfloat16)
    fine = (nums - coarse.astype(jnp.float32)).astype(jnp.bfloat16)
    nums = jnp.concatenate([coarse, fine, coarse, fine], axis=0)

    def rates(start, count):
        found = jnp.dot(
            abuf[start : start + count].reshape(count * 16, 256), nums, preferred_element_type=jnp.float32
        )
        tbuf[start : start + count] = found.reshape(count, 16, 128)

    def gain(z):
        acc = [[None] * 2 for _ in range(8)]
        for i in range(TRC):
            m = [recv2[i, 0:8, :], recv2[i, 8:16, :]]
            for b in range(8):
                t = jnp.broadcast_to(tbuf[1 + 8 * z + b, i : i + 1, :], (8, 128))
                for h in range(2):
                    term = t * m[h]
                    acc[b][h] = term if acc[b][h] is None else acc[b][h] + term
        for x in range(SIDE):
            g = 4 * x + z
            rec = jnp.broadcast_to(rbuf[g : g + 1, :], (8, 128))
            for h in range(2):
                even, odd = acc[2 * x][h], acc[2 * x + 1][h]
                gained = jnp.where(low, even, odd) + pltpu.roll(jnp.where(low, odd, even), 64, 1)
                send3[g, 8 * h : 8 * h + 8, :] = (recv2[g, 8 * h : 8 * h + 8, :] + gained) * rec
        for i in (2, 1, 3, 0):
            spread(send3, recv3, s3_sem, r3_sem, 4 * lax.rem(x_me + i, SIDE) + z).start()

    rates(0, 9)
    rbuf[...] = 1.0 / (1.0 + tbuf[0])
    for z in range(SIDE):
        if z < SIDE - 1:
            rates(9 + 8 * z, 8)
        gain(z)

    for dest in others:
        share(dest).wait_send()
    for side in range(2):
        halo(side).wait_send()
        for i in range(2):
            moved_halo(side, i).wait_send()
    for dest in range(TRC):
        spread(send2, recv2, s2_sem, r2_sem, dest).wait_send()
    for dest in range(TRC):
        spread(send3, recv3, s3_sem, r3_sem, dest).wait_send()
    for k in (3, 2, 1, 0):
        x = plane(k)
        for z in range(SIDE):
            arrived(recv3, r3_sem, s3_sem, 4 * x + z).wait_recv()
        for i in range(2):
            r = 2 * x + i
            for h in range(2):
                c0, c1 = recv3[2 * r, 8 * h : 8 * h + 8, :], recv3[2 * r + 1, 8 * h : 8 * h + 8, :]
                out[pl.ds(64 * h + r, 8, stride=8), :] = jnp.where(low, c0, pltpu.roll(c1, 64, 1))
                out[pl.ds(128 + 64 * h + r, 8, stride=8), :] = jnp.where(low, pltpu.roll(c0, 64, 1), c1)


def solution(mesh):
    n_tile = mesh.shape["tile"]
    f32, i32, bf16 = jnp.float32, jnp.int32, jnp.bfloat16
    anywhere = pl.BlockSpec(memory_space=pltpu.HBM)

    def on_device(tracers, courant, shear, offsets, seam_flips, kernel, coag_target):
        result = pl.pallas_call(
            functools.partial(body, n_tile),
            out_shape=jax.ShapeDtypeStruct((256, 128), f32),
            in_specs=[anywhere] * 7,
            out_specs=pl.BlockSpec(memory_space=pltpu.VMEM),
            scratch_shapes=[
                pltpu.VMEM((256, 128), f32),
                pltpu.VMEM((24, 8), f32),
                pltpu.VMEM((24, 8), f32),
                pltpu.VMEM((24, 128), i32),
                pltpu.SMEM((32,), i32),
                pltpu.VMEM((32, 32), f32),
                pltpu.VMEM((32, 32), i32),
                pltpu.VMEM((24, 128), f32),
                pltpu.VMEM((2, 128), f32),
                pltpu.VMEM((TRC, 2, 128), f32),
                pltpu.VMEM((50, 8, 128), f32),
                pltpu.VMEM((16, 32, 128), f32),
                pltpu.VMEM((16, 32, 128), f32),
                pltpu.VMEM((4, 32, 128), f32),
                pltpu.VMEM((TRC, 16, 128), f32),
                pltpu.VMEM((TRC, 16, 128), f32),
                pltpu.VMEM((BINS + 1, 16, 256), bf16),
                pltpu.VMEM((16, 128), f32),
                pltpu.VMEM((BINS + 1, 16, 128), f32),
                pltpu.VMEM((16, 128), f32),
                pltpu.VMEM((TRC, 16, 128), f32),
                pltpu.VMEM((TRC, 16, 128), f32),
                pltpu.SemaphoreType.DMA((7,)),
                pltpu.SemaphoreType.DMA((3, 2)),
                pltpu.SemaphoreType.DMA((3, 2)),
                pltpu.SemaphoreType.DMA((TRC,)),
                pltpu.SemaphoreType.DMA((TRC,)),
                pltpu.SemaphoreType.REGULAR,
                pltpu.SemaphoreType.DMA((TRC,)),
                pltpu.SemaphoreType.DMA((TRC,)),
                pltpu.SemaphoreType.DMA((TRC,)),
                pltpu.SemaphoreType.DMA((TRC,)),
            ],
            compiler_params=pltpu.CompilerParams(
                collective_id=0, has_side_effects=True, vmem_limit_bytes=48 * 1024 * 1024
            ),
        )(
            *(
                pltpu.with_memory_space_constraint(v, pltpu.HBM)
                for v in (
                    tracers.reshape(256, 128), courant.reshape(24, 8), shear.reshape(24, 8),
                    offsets.reshape(24, 128), seam_flips, kernel, coag_target,
                )
            ),
        )
        return result.reshape(32, 4, 2, 128)

    return jax.shard_map(
        on_device,
        mesh=mesh,
        in_specs=(
            P("trc", "tile", None, None),
            P(None, "tile", None, "trc"),
            P(None, "tile", None, "trc"),
            P(None, "tile", None, None),
            P(),
            P(),
            P(),
        ),
        out_specs=P("trc", "tile", None, None),
        check_vma=False,
    )
```

```python
import functools

import jax
import jax.numpy as jnp
from jax import lax
from jax.experimental import pallas as pl
from jax.experimental.pallas import tpu as pltpu
from jax.sharding import PartitionSpec as P

BINS = 32
COMPS = 16
ITER = 3
TRC = 16
SIDE = 4
MESH = pl.DeviceIdType.MESH
EXACT = lax.Precision.HIGHEST


def taps(f, lower):
    p0 = -f * (f - 1.0) * (f - 2.0) / 6.0
    p1 = (f + 1.0) * (f - 1.0) * (f - 2.0) / 2.0
    p2 = -(f + 1.0) * f * (f - 2.0) / 2.0
    p3 = (f + 1.0) * f * (f - 1.0) / 6.0
    zero = jnp.zeros_like(f)
    return [
        jnp.where(lower, p0, zero),
        jnp.where(lower, p1, p0),
        jnp.where(lower, p2, p1),
        jnp.where(lower, p3, p2),
        jnp.where(lower, zero, p3),
    ]


def transport(src, wbuf, x, steps=range(5), out=None):
    for b in range(5):
        acc = [[None] * 4, [None] * 4]
        for a in steps:
            for level in range(2):
                q = [src[2 * x + 2 * a + level, pl.ds(8 * g, 8), :] for g in range(4)]
                for l in range(2):
                    w = wbuf[(b * 5 + a) * 2 + level, pl.ds(2 * x + l, 1), :]
                    w = jnp.broadcast_to(w, (8, 128))
                    for g in range(4):
                        term = w * q[g]
                        acc[l][g] = term if acc[l][g] is None else acc[l][g] + term
        if b != 2:
            acc = [[pltpu.roll(v, (2 - b) % 128, 1) for v in row] for row in acc]
        out = acc if out is None else [[o + v for o, v in zip(r, s)] for r, s in zip(out, acc)]
    return out


def body(
    n_tile, tr, co, sh, of, fi, ke, ct, out,
    tin, cin, sin, oin, fl, kin, ctin, fpad, fsend, frecv, wbuf, src1, src2, part,
    send2, recv2, abuf, nbuf, tbuf, rbuf, send3, recv3,
    in_sem, hs_sem, hr_sem, fs_sem, fr_sem, known_sem, s2_sem, r2_sem, s3_sem, r3_sem,
):
    tile, me = lax.axis_index("tile"), lax.axis_index("trc")
    x_me, z_me = me // SIDE, lax.rem(me, SIDE)
    prev = lax.rem(tile + n_tile - 1, n_tile)
    after = lax.rem(tile + 1, n_tile)

    quad = lax.rem(tile, 4)
    side_far = lax.rem(quad, 2)
    partner = tile + 2 - 4 * (quad // 2)

    def plane(k):
        return lax.rem(x_me + 6 - k + 3 * (k // 2) + 2 * (k // 3), SIDE)

    others = [4 * plane(k) + lax.rem(z_me + i, SIDE) for k in range(SIDE) for i in (2, 1, 3, 0)][:-1]
    barrier = pltpu.get_barrier_semaphore()
    for dest in others:
        pl.semaphore_signal(barrier, inc=1, device_id=(tile, dest), device_id_type=MESH)
    for t in (prev, after):
        pl.semaphore_signal(barrier, inc=1, device_id=(t, me), device_id_type=MESH)

    loads = [
        pltpu.make_async_copy(s, d, in_sem.at[i])
        for i, (s, d) in enumerate(
            ((co, cin), (sh, sin), (tr, tin), (of, oin), (ke, kin), (ct, ctin), (fi, fl))
        )
    ]
    for load in loads:
        load.start()

    lane = lax.broadcasted_iota(jnp.int32, (8, 128), 1)
    sub = lax.broadcasted_iota(jnp.int32, (8, 128), 0)
    low = lane < 64

    fpad[...] = jnp.zeros_like(fpad)
    loads[0].wait()
    loads[1].wait()
    c, s = cin[...], sin[...]
    f = jnp.full(c.shape, 0.5, jnp.float32)
    for _ in range(ITER):
        f = jax.nn.sigmoid(c + s * (f - 0.5))
    fpad[:, 0:8] = f
    zero = jnp.zeros((8, 128), jnp.float32)
    rows = []
    for packed in (fpad[0:8] + pltpu.roll(fpad[8:16], 8, 1), fpad[16:24]):
        for bit in (1, 2, 4):
            packed = jnp.where(lax.rem(sub // bit, 2) == 1, pltpu.roll(packed, 128 - 16 * bit, 1), packed)
        packed = pltpu.roll(packed, me * 8, 1)
        rows.append(jnp.sum(packed, axis=0, keepdims=True))
    top, bottom = rows
    fsend[0:1, :] = top
    fsend[1:2, :] = bottom
    frecv[me, 0:1, :] = top
    frecv[me, 1:2, :] = bottom

    loads[2].wait()
    for r in range(8):
        for g in range(4):
            src1[4 + r, pl.ds(8 * g, 8), :] = tin[pl.ds(64 * g + r, 8, stride=8), :]

    pl.semaphore_wait(barrier, TRC + 1)

    def halo(side):
        return pltpu.make_async_remote_copy(
            src_ref=src1.at[pl.ds(4 + 4 * side, 4)],
            dst_ref=src1.at[pl.ds(12 - 12 * side, 4)],
            send_sem=hs_sem.at[0, side],
            recv_sem=hr_sem.at[0, side],
            device_id=((prev, after)[side], me),
            device_id_type=MESH,
        )

    def moved_halo(side, i):
        return pltpu.make_async_remote_copy(
            src_ref=src2.at[pl.ds(4 + 4 * side + 2 * i, 2)],
            dst_ref=src2.at[pl.ds(12 - 12 * side + 2 * i, 2)],
            send_sem=hs_sem.at[1 + i, side],
            recv_sem=hr_sem.at[1 + i, side],
            device_id=(lax.rem(tile + n_tile - 1 + 2 * side, n_tile), me),
            device_id_type=MESH,
        )

    def share(dest):
        return pltpu.make_async_remote_copy(
            src_ref=fsend, dst_ref=frecv.at[me], send_sem=fs_sem.at[dest], recv_sem=fr_sem.at[me],
            device_id=(tile, dest), device_id_type=MESH,
        )

    def spread(src, dst, s_sem, r_sem, dest):
        return pltpu.make_async_remote_copy(
            src_ref=src.at[dest], dst_ref=dst.at[me], send_sem=s_sem.at[dest], recv_sem=r_sem.at[me],
            device_id=(partner, dest), device_id_type=MESH,
        )

    def arrived(dst, r_sem, s_sem, source):
        return pltpu.make_async_remote_copy(
            src_ref=dst.at[source], dst_ref=dst.at[source], send_sem=s_sem.at[source],
            recv_sem=r_sem.at[source], device_id=(tile, source), device_id_type=MESH,
        )

    for z in (3, 2, 1, 0):
        for i in (2, 1, 3, 0):
            dest = 4 * lax.rem(x_me + i, SIDE) + z

            @pl.when(dest != me)
            def _(dest=dest):
                share(dest).start()

    halo(0).start()
    halo(1).start()

    loads[4].wait()
    loads[5].wait()
    spot = lax.broadcasted_iota(jnp.int32, (32, 256), 1)
    j = lax.broadcasted_iota(jnp.int32, (32, 256), 0)
    at = lax.rem(j, 2) * 16 + j // 2
    rate = jnp.zeros((16, 256), jnp.float32)
    target = jnp.zeros((16, 256), jnp.float32)
    for p in range(2):
        place = (lax.rem(spot, 64) == at + 32 * p).astype(jnp.float32)
        rate += jnp.dot(kin[pl.ds(p, 16, stride=2), :], place, precision=EXACT, preferred_element_type=jnp.float32)
        target += jnp.dot(
            ctin[pl.ds(p, 16, stride=2), :].astype(jnp.float32), place, precision=EXACT,
            preferred_element_type=jnp.float32,
        )
    coarse = rate.astype(jnp.bfloat16).astype(jnp.float32)
    rate = jnp.where(lax.broadcasted_iota(jnp.int32, (16, 256), 1) < 128, coarse, rate - coarse)

    def fill(b, carry):
        hit = jnp.abs(target - b.astype(jnp.float32)) < 0.5
        abuf[1 + 8 * (lax.rem(b, 8) // 2) + 2 * (b // 8) + lax.rem(b, 2)] = jnp.where(hit, rate, 0.0).astype(jnp.bfloat16)
        return carry

    lax.fori_loop(0, BINS, fill, 0)
    abuf[0] = rate.astype(jnp.bfloat16)

    mirror = 127 - lane
    loads[6].wait()

    def turn(buf, side, rows=range(4)):
        turned = jnp.full((8, 128), fl[lax.rem(tile + side, n_tile)], jnp.int32) == 1
        for i in rows:
            for g in range(4):
                at = (12 * side + i, pl.ds(8 * g, 8), slice(None))
                v = buf[at]
                buf[at] = jnp.where(turned, jnp.take_along_axis(v, mirror, axis=1), v)

    for side in range(2):
        halo(1 - side).wait_recv()
        turn(src1, side)

    loads[3].wait()
    place = lax.rem(lane // 8 + 2 * sub, 16)
    spots = [place, lax.rem(place + 15, 16), place]
    frac = [zero, zero, zero]
    for source in [me] + others[::-1]:
        if source is not me:
            arrived(frecv, fr_sem, fs_sem, source).wait_recv()
        rows = [jnp.broadcast_to(frecv[source, i : i + 1, :], (8, 128)) for i in (0, 0, 1)]
        frac = [jnp.where(spots[d] == source, rows[d], frac[d]) for d in range(3)]

    inner = (quad + 1) // 2 == 1

    @pl.when(inner)
    def _():
        pl.semaphore_signal(
            known_sem, inc=1, device_id=(lax.rem(tile + n_tile - 1 + 2 * side_far, n_tile), me), device_id_type=MESH
        )

    frac[1] = pltpu.roll(frac[1], 120, 1)
    weights = []
    for d in range(3):
        fd = pltpu.roll(frac[d], 0, 1, stride=16, stride_axis=0)
        weights.append(taps(fd, oin[8 * d : 8 * d + 8, :] == -1))
    cross, levels, along = weights
    upper = lax.rem(sub, 2) == 1
    level0 = levels[0] + levels[1] + jnp.where(upper, zero, levels[2])
    level1 = levels[3] + levels[4] + jnp.where(upper, levels[2], zero)
    for a in range(5):
        for level, lw in enumerate((level0, level1)):
            pair = cross[a] * lw
            for b in range(5):
                w = pair * along[b]
                if b != 2:
                    w = pltpu.roll(w, (b - 2) % 128, 1)
                wbuf[(b * 5 + a) * 2 + level] = w

    def first(k, carry):
        side = lax.rem(side_far + k // 2, 2)
        x = 2 * side + lax.rem(k, 2)
        moved = transport(src1, wbuf, x)
        for l in range(2):
            for g in range(4):
                src2[4 + 2 * x + l, pl.ds(8 * g, 8), :] = moved[l][g]
        moved_halo(side, lax.rem(k, 2)).start()
        return carry

    lax.fori_loop(0, 4, first, 0)

    def rim(side):
        for i in range(2):
            moved_halo(1 - side, i).wait_recv()
        turn(src2, side)

    zs = [lax.rem(z_me + 1 + quad // 2 + i, SIDE) for i in range(SIDE)]

    def pack(moved, x):
        for l in range(2):
            for g in range(2):
                even, odd = moved[l][g], moved[l][2 + g]
                at = pl.ds(8 * g, 8)
                send2[4 * x + 2 * l, at, :] = jnp.where(low, even, pltpu.roll(odd, 64, 1))
                send2[4 * x + 2 * l + 1, at, :] = jnp.where(low, pltpu.roll(even, 64, 1), odd)

    def leave(side):
        near = lax.rem(x_me + 5 - 2 * side, SIDE) // 2
        for k in range(2):
            x = 2 * side + lax.rem(1 - near + k, 2)
            for i in range(SIDE):
                spread(send2, recv2, s2_sem, r2_sem, 4 * x + zs[i]).start()

    def early(k, carry):
        x = 2 * (1 - side_far) + k
        pack(transport(src2, wbuf, x), x)
        return carry

    rim(1 - side_far)
    lax.fori_loop(0, 2, early, 0)

    steps = [4 * side_far + n * (1 - 2 * side_far) for n in range(5)]
    cells = ((3 * side_far, 2), (1 + side_far, 1))
    for i, (x, reach) in enumerate(cells):
        moved = transport(src2, wbuf, x, steps[reach:])
        for l in range(2):
            for g in range(4):
                part[2 * i + l, pl.ds(8 * g, 8), :] = moved[l][g]

    @pl.when(inner)
    def _():
        pl.semaphore_wait(known_sem, 1)

    for i in range(2):
        moved_halo(1 - side_far, i).wait_recv()
        turn(src2, side_far, (2 * i, 2 * i + 1))
    for i, (x, reach) in enumerate(cells):
        moved = [[part[2 * i + l, pl.ds(8 * g, 8), :] for g in range(4)] for l in range(2)]
        pack(transport(src2, wbuf, x, steps[:reach], moved), x)
    for half in range(2):
        for k in range(SIDE):
            for i in range(2):
                spread(send2, recv2, s2_sem, r2_sem, 4 * plane(k) + zs[2 * half + i]).start()

    sources = [4 * plane(k) + lax.rem(z_me + quad // 2 + 3 + i, SIDE) for k in (3, 2, 1, 0) for i in range(SIDE)]
    for k in range(SIDE):
        group = sources[SIDE * k : SIDE * k + SIDE]
        for source in group:
            arrived(recv2, r2_sem, s2_sem, source).wait_recv()
        for source in group:
            nbuf[pl.ds(source, 1), :] = jnp.sum(jnp.abs(recv2[source]), axis=0, keepdims=True)
    number = nbuf[...]
    low16 = lax.broadcasted_iota(jnp.int32, (16, 128), 1) < 64
    other = pltpu.roll(number, 64, 1)
    none = jnp.zeros_like(number)
    nums = jnp.concatenate(
        [
            jnp.where(low16, number, none),
            jnp.where(low16, other, none),
            jnp.where(low16, none, other),
            jnp.where(low16, none, number),
        ],
        axis=0,
    )
    coarse = nums.astype(jnp.bfloat16)
    fine = (nums - coarse.astype(jnp.float32)).astype(jnp.bfloat16)
    nums = jnp.concatenate([coarse, fine, coarse, fine], axis=0)

    def rates(start, count):
        found = jnp.dot(
            abuf[start : start + count].reshape(count * 16, 256), nums, preferred_element_type=jnp.float32
        )
        tbuf[start : start + count] = found.reshape(count, 16, 128)

    def gain(z):
        acc = [[None] * 2 for _ in range(8)]
        for i in range(TRC):
            m = [recv2[i, 0:8, :], recv2[i, 8:16, :]]
            for b in range(8):
                t = jnp.broadcast_to(tbuf[1 + 8 * z + b, i : i + 1, :], (8, 128))
                for h in range(2):
                    term = t * m[h]
                    acc[b][h] = term if acc[b][h] is None else acc[b][h] + term
        for x in range(SIDE):
            g = 4 * x + z
            rec = jnp.broadcast_to(rbuf[g : g + 1, :], (8, 128))
            for h in range(2):
                even, odd = acc[2 * x][h], acc[2 * x + 1][h]
                gained = jnp.where(low, even, odd) + pltpu.roll(jnp.where(low, odd, even), 64, 1)
                send3[g, 8 * h : 8 * h + 8, :] = (recv2[g, 8 * h : 8 * h + 8, :] + gained) * rec
        for i in (2, 1, 3, 0):
            spread(send3, recv3, s3_sem, r3_sem, 4 * lax.rem(x_me + i, SIDE) + z).start()

    rates(0, 9)
    rbuf[...] = 1.0 / (1.0 + tbuf[0])
    for z in range(SIDE):
        if z < SIDE - 1:
            rates(9 + 8 * z, 8)
        gain(z)

    for dest in others:
        share(dest).wait_send()
    for side in range(2):
        halo(side).wait_send()
        for i in range(2):
            moved_halo(side, i).wait_send()
    for dest in range(TRC):
        spread(send2, recv2, s2_sem, r2_sem, dest).wait_send()
    for dest in range(TRC):
        spread(send3, recv3, s3_sem, r3_sem, dest).wait_send()
    for k in (3, 2, 1, 0):
        x = plane(k)
        for z in range(SIDE):
            arrived(recv3, r3_sem, s3_sem, 4 * x + z).wait_recv()
        for i in range(2):
            r = 2 * x + i
            for h in range(2):
                c0, c1 = recv3[2 * r, 8 * h : 8 * h + 8, :], recv3[2 * r + 1, 8 * h : 8 * h + 8, :]
                out[pl.ds(64 * h + r, 8, stride=8), :] = jnp.where(low, c0, pltpu.roll(c1, 64, 1))
                out[pl.ds(128 + 64 * h + r, 8, stride=8), :] = jnp.where(low, pltpu.roll(c0, 64, 1), c1)


def solution(mesh):
    n_tile = mesh.shape["tile"]
    f32, i32, bf16 = jnp.float32, jnp.int32, jnp.bfloat16
    anywhere = pl.BlockSpec(memory_space=pltpu.HBM)

    def on_device(tracers, courant, shear, offsets, seam_flips, kernel, coag_target):
        result = pl.pallas_call(
            functools.partial(body, n_tile),
            out_shape=jax.ShapeDtypeStruct((256, 128), f32),
            in_specs=[anywhere] * 7,
            out_specs=pl.BlockSpec(memory_space=pltpu.VMEM),
            scratch_shapes=[
                pltpu.VMEM((256, 128), f32),
                pltpu.VMEM((24, 8), f32),
                pltpu.VMEM((24, 8), f32),
                pltpu.VMEM((24, 128), i32),
                pltpu.SMEM((32,), i32),
                pltpu.VMEM((32, 32), f32),
                pltpu.VMEM((32, 32), i32),
                pltpu.VMEM((24, 128), f32),
                pltpu.VMEM((2, 128), f32),
                pltpu.VMEM((TRC, 2, 128), f32),
                pltpu.VMEM((50, 8, 128), f32),
                pltpu.VMEM((16, 32, 128), f32),
                pltpu.VMEM((16, 32, 128), f32),
                pltpu.VMEM((4, 32, 128), f32),
                pltpu.VMEM((TRC, 16, 128), f32),
                pltpu.VMEM((TRC, 16, 128), f32),
                pltpu.VMEM((BINS + 1, 16, 256), bf16),
                pltpu.VMEM((16, 128), f32),
                pltpu.VMEM((BINS + 1, 16, 128), f32),
                pltpu.VMEM((16, 128), f32),
                pltpu.VMEM((TRC, 16, 128), f32),
                pltpu.VMEM((TRC, 16, 128), f32),
                pltpu.SemaphoreType.DMA((7,)),
                pltpu.SemaphoreType.DMA((3, 2)),
                pltpu.SemaphoreType.DMA((3, 2)),
                pltpu.SemaphoreType.DMA((TRC,)),
                pltpu.SemaphoreType.DMA((TRC,)),
                pltpu.SemaphoreType.REGULAR,
                pltpu.SemaphoreType.DMA((TRC,)),
                pltpu.SemaphoreType.DMA((TRC,)),
                pltpu.SemaphoreType.DMA((TRC,)),
                pltpu.SemaphoreType.DMA((TRC,)),
            ],
            compiler_params=pltpu.CompilerParams(
                collective_id=0, has_side_effects=True, vmem_limit_bytes=48 * 1024 * 1024
            ),
        )(
            *(
                pltpu.with_memory_space_constraint(v, pltpu.HBM)
                for v in (
                    tracers.reshape(256, 128), courant.reshape(24, 8), shear.reshape(24, 8),
                    offsets.reshape(24, 128), seam_flips, kernel, coag_target,
                )
            ),
        )
        return result.reshape(32, 4, 2, 128)

    return jax.shard_map(
        on_device,
        mesh=mesh,
        in_specs=(
            P("trc", "tile", None, None),
            P(None, "tile", None, "trc"),
            P(None, "tile", None, "trc"),
            P(None, "tile", None, None),
            P(),
            P(),
            P(),
        ),
        out_specs=P("trc", "tile", None, None),
        check_vma=False,
    )
```
